32 devices in a mesh: wave: 8 (over z, y), lev: 4 (over x, core).
Axes of the slice: x: 2, y: 2, z: 4, core: 2. Of those that a mesh axis runs over, the one named last changes fastest.
Arguments:
- spectral: bfloat16 [2, 16, 640, 1281], P(None, 'lev', 'wave'), may hold values from -6 to 6
- legendre: bfloat16 [640, 1281, 64], P(('wave', 'lev')), may hold values from -0.0048828125 to 0.0048828125
- wave_table: int32 [640], replicated, may hold values from 0 to 639, each once
- courant_lon: float32 [16, 64, 5120], P('lev', 'wave'), may hold values from -0.35 to 0.35
- courant_lat: float32 [16, 64, 5120], P('lev', 'wave'), may hold values from -0.35 to 0.35
Outputs:
- tracer: float32 [16, 64, 5120], P('lev', 'wave')
The draws below stay inside these ranges and needn't reach their ends.
Inputs may be any that keep to these rules, and one draw needn't show every extreme that they name: A permutation of the pairs: slot s carries wavenumbers wave_table[s] and 1279 - wave_table[s].
All inputs are finite; a program needn't handle non-finite values.
Results may differ from the reference program's by a relative error of at most 0.003.
Values may be sent and summed in bfloat16 or wider, within the bound.
No kernel may reach another device: no remote copies, remote signals or barrier semaphores. Data moves between devices by JAX's collectives and lax.ppermute only.
A program may use at most 64 MiB of HBM per device.

```python
import jax
import jax.numpy as jnp
from jax import lax

M = 1280
NLON = 5120
K = 1281
PAIRS = 640
LATW = 64
LEVELS = 16
PASSES = 4


def block_levels(key, dims, shards, least, top_value):
    level, own = 1.0, jax.random.fold_in(key, 6)
    for position, shards_of in shards:
        heights = jnp.exp(jax.random.uniform(jax.random.fold_in(own, position), (shards_of,), jnp.float32, least / len(shards), top_value / len(shards)))
        level = level * jnp.repeat(heights, dims[position] // shards_of).reshape([-1 if axis == position else 1 for axis in range(len(dims))])
    return level


def scatter_about(key, dims, deviation, limit, pieces=(), dtype=jnp.bfloat16):
    array = deviation * jax.random.normal(key, dims, jnp.float32)
    if pieces:
        array = array * block_levels(key, dims, pieces, -0.22, 0.18)
    return jnp.clip(array, -limit, limit).astype(dtype)


def setup_inputs(seed: int = 0) -> dict:
    splits = jax.random.split(jax.random.key(seed), 6)
    return {
        "spectral": scatter_about(splits[0], (2, LEVELS, PAIRS, K), 1.0, 6.0, ((1, 4), (2, 8))),
        "legendre": scatter_about(splits[1], (PAIRS, K, LATW), (K * M) ** -0.5, 0.0048828125, ((0, 32),)),
        "wave_table": jax.random.permutation(splits[2], PAIRS).astype(jnp.int32),
        "courant_lon": jnp.clip(jax.random.uniform(splits[3], (LEVELS, LATW, NLON), jnp.float32, -0.35, 0.35) * block_levels(splits[3], (LEVELS, LATW, NLON), ((0, 4), (1, 8)), -0.4, 0.0), -0.35, 0.35),
        "courant_lat": jnp.clip(jax.random.uniform(splits[4], (LEVELS, LATW, NLON), jnp.float32, -0.35, 0.35) * block_levels(splits[4], (LEVELS, LATW, NLON), ((0, 4), (1, 8)), -0.4, 0.0), -0.35, 0.35),
    }


def donor_flux(left_side, right_side, speed):
    return jnp.maximum(speed, 0.0) * left_side + jnp.minimum(speed, 0.0) * right_side


def from_west(field):
    return jnp.roll(field, 1, axis=-1)


def from_east(field):
    return jnp.roll(field, -1, axis=-1)


def floored_ratio(numerator, denominator):
    return numerator / jnp.maximum(denominator, 1.0)


def mpdata_pass(tracer_rows, speed_lon, speed_lat, inside):
    flux_lon = donor_flux(from_west(tracer_rows), tracer_rows, speed_lon)
    flux_lat = donor_flux(tracer_rows[..., :-1, :], tracer_rows[..., 1:, :], speed_lat[..., 1:, :])
    upwind = tracer_rows[..., 1:-1, :] - (from_east(flux_lon) - flux_lon)[..., 1:-1, :] - (flux_lat[..., 1:, :] - flux_lat[..., :-1, :])
    upwind = jnp.where(inside[1:-1, None], upwind, 0.0)
    west_side = from_west(upwind)
    centre = upwind[..., 1:-1, :]
    left_cell = west_side[..., 1:-1, :]
    upper_row = upwind[..., 2:, :]
    upper_west = west_side[..., 2:, :]
    lower_row = upwind[..., :-2, :]
    lower_west = west_side[..., :-2, :]
    grad_lon = floored_ratio(centre - left_cell, jnp.abs(centre) + jnp.abs(left_cell))
    cross_lon = 0.5 * floored_ratio(upper_row + upper_west - lower_row - lower_west, jnp.abs(upper_row) + jnp.abs(upper_west) + jnp.abs(lower_row) + jnp.abs(lower_west))
    speed_x = speed_lon[..., 2:-2, :]
    lat_west = from_west(speed_lat)
    mean_lat = 0.25 * (speed_lat[..., 2:-2, :] + speed_lat[..., 3:-1, :] + lat_west[..., 2:-2, :] + lat_west[..., 3:-1, :])
    anti_lon = (jnp.abs(speed_x) - speed_x * speed_x) * grad_lon - speed_x * mean_lat * cross_lon
    above_row = upwind[..., 1:, :]
    below_row = upwind[..., :-1, :]
    grad_lat = floored_ratio(above_row - below_row, jnp.abs(above_row) + jnp.abs(below_row))
    above_east = from_east(above_row)
    below_east = from_east(below_row)
    above_west = from_west(above_row)
    below_west = from_west(below_row)
    cross_lat = 0.5 * floored_ratio(above_east + below_east - above_west - below_west, jnp.abs(above_east) + jnp.abs(below_east) + jnp.abs(above_west) + jnp.abs(below_west))
    speed_y = speed_lat[..., 2:-1, :]
    lon_east = from_east(speed_lon)
    mean_lon = 0.25 * (speed_lon[..., 2:-1, :] + lon_east[..., 2:-1, :] + speed_lon[..., 1:-2, :] + lon_east[..., 1:-2, :])
    anti_lat = (jnp.abs(speed_y) - speed_y * speed_y) * grad_lat - speed_y * mean_lon * cross_lat
    corr_lon = donor_flux(left_cell, centre, anti_lon)
    corr_lat = donor_flux(below_row, above_row, anti_lat)
    second = centre - (from_east(corr_lon) - corr_lon) - (corr_lat[..., 1:, :] - corr_lat[..., :-1, :])
    return jnp.where(inside[2:-2, None], second, 0.0)


def reference(spectral, legendre, wave_table, courant_lon, courant_lat):
    def one_slot(slot_items):
        spectra, table_rows, pair_id = slot_items
        lower_part = jnp.arange(K) < M - pair_id
        nothing = jnp.zeros((), jnp.bfloat16)
        halves = jnp.stack([jnp.where(lower_part, spectra, nothing), jnp.where(lower_part, nothing, spectra)], 0)
        return jnp.einsum("wrlk,kt->wrlt", halves.astype(jnp.float32), table_rows.astype(jnp.float32), precision=lax.Precision.HIGHEST)

    by_slot = jnp.transpose(spectral, (2, 0, 1, 3))
    terms = lax.map(one_slot, (by_slot, legendre, wave_table))
    coefficients = lax.optimization_barrier(terms.astype(jnp.bfloat16)).astype(jnp.float32)
    numbers = jnp.stack([wave_table, M - 1 - wave_table], 1).reshape(-1).astype(jnp.int32)
    placed = jnp.zeros((M, 2, LEVELS, LATW), jnp.float32).at[numbers].set(coefficients.reshape(M, 2, LEVELS, LATW))
    real_part = jnp.transpose(placed[:, 0], (1, 2, 0))
    imag_part = jnp.transpose(placed[:, 1], (1, 2, 0))
    spectrum = lax.complex(real_part, imag_part)
    spectrum = jnp.pad(spectrum, ((0, 0), (0, 0), (0, NLON // 2 + 1 - M)))
    grid = (jnp.fft.irfft(spectrum, n=NLON, axis=-1) * NLON).astype(jnp.float32)

    def advect(level_items):
        field, speed_lon, speed_lat = level_items
        row_index = jnp.arange(-2, LATW + 2)
        inside = (row_index >= 0) & (row_index < LATW)
        padded_lon = jnp.pad(speed_lon, ((2, 2), (0, 0)))
        padded_lat = jnp.pad(speed_lat, ((2, 2), (0, 0)))
        for number in range(PASSES):
            field = mpdata_pass(jnp.pad(field, ((2, 2), (0, 0))), padded_lon, padded_lat, inside)
        return field

    return lax.map(advect, (grid, courant_lon, courant_lat))
```

```python
import functools
import math

import jax
import jax.numpy as jnp
import ml_dtypes
import numpy as np
from jax import lax
from jax.experimental import pallas as pl
from jax.experimental.pallas import tpu as pltpu
from jax.sharding import PartitionSpec as P

PASSES = 4
HALO = 2 * PASSES
SUB = 8
LANES = 128
NEAR = 2 * LANES
F32 = jnp.float32
BF16 = jnp.bfloat16


def params(mib):
    return pltpu.CompilerParams(vmem_limit_bytes=mib << 20)


def lane_index():
    return lax.broadcasted_iota(jnp.int32, (SUB, LANES), 1)


def pack_kernel(count, x_ref, *refs):
    outs, turned = refs[:count], refs[count]
    slots, degrees = x_ref.shape[1:]
    own = slots // count
    me = lax.axis_index("lev")

    def gather(first, rows):
        for lo in range(0, degrees, LANES):
            hi = min(lo + LANES, degrees)
            tile = jnp.stack(
                [x_ref[i, first : first + rows, lo:hi].astype(F32) for i in range(SUB)], 0
            )
            turned[first : first + rows, :, lo:hi] = jnp.swapaxes(tile, 0, 1)

    for first in range(0, slots, SUB):
        gather(first, SUB)
    for step, out in enumerate(outs):
        start = (me ^ step) * own

        def pair(i, carry, out=out, start=start):
            second = jnp.minimum(start + 2 * i + 1, slots - 1)
            both = [turned[start + 2 * i], turned[second]]
            out[i] = jnp.concatenate(both, 0).astype(BF16)
            return carry

        lax.fori_loop(0, out.shape[0], pair, 0)


def pack(spectral, count):
    parts, levels, slots, degrees = spectral.shape
    out = jax.ShapeDtypeStruct((-(-slots // count // 2), 2 * SUB, degrees), BF16)
    return pl.pallas_call(
        functools.partial(pack_kernel, count),
        out_shape=[out] * count,
        scratch_shapes=[pltpu.VMEM((slots, SUB, degrees), F32)],
        compiler_params=params(40),
        name="pack",
    )(spectral.reshape(parts * levels, slots, degrees))


def legendre_kernel(steps, bands, waves, pad, pairs_ref, *refs):
    count = len(steps)
    blocks, table = refs[:count], refs[count]
    outs = refs[count + 1 : 2 * count + 1]
    sums = refs[2 * count + 1]
    own, degrees, lats = table.shape
    wide = sums.shape[-1]
    band = lats // bands
    pieces = band // SUB + 2
    if wide > lats:
        sums[...] = jnp.zeros_like(sums)
    elif 2 * own < pad:
        sums[:, 2 * own :] = jnp.zeros((count, pad - 2 * own, SUB, wide), F32)

    def pair(i, carry):
        rows = jnp.concatenate([block[i] for block in blocks], 0).astype(F32)
        row = lax.broadcasted_iota(jnp.int32, rows.shape, 0) % (2 * SUB)
        degree = lax.broadcasted_iota(jnp.int32, rows.shape, 1)
        second = jnp.minimum(2 * i + 1, own - 1)
        bound = waves - jnp.where(row < SUB, pairs_ref[2 * i], pairs_ref[second])
        low = jnp.where(degree < bound, rows, 0.0)
        both = jnp.concatenate([low, rows - low], 0).astype(BF16)
        for j in range(2):
            got = jnp.dot(both, table[second if j else 2 * i], preferred_element_type=F32)
            for half in range(2):
                for d in range(count):
                    first = (half * count + d) * 2 * SUB + j * SUB
                    sums[d, 4 * i + 2 * j + half, :, :lats] = got[first : first + SUB]
        return carry

    lax.fori_loop(0, blocks[0].shape[0], pair, 0)
    lane = lax.broadcasted_iota(jnp.int32, (SUB, wide), 1)
    for d in range(count):
        tiles = [
            [jnp.swapaxes(sums[d, 8 * g : 8 * g + 8, :, k : k + LANES], 0, 1) for k in range(0, wide, LANES)]
            for g in range(pad // SUB)
        ]
        wides = []
        for i in range(SUB):
            tall = []
            for piece in range(pieces):
                shift = SUB - SUB * piece
                for g in range(pad // SUB):
                    value = jnp.concatenate([tile[i] for tile in tiles[g]], 1)
                    if shift:
                        value = pltpu.roll(value, shift % wide, 1)
                        value = jnp.where((lane >= shift) & (lane < lats + shift), value, 0.0)
                    tall.append(value)
            spare = LANES - pieces * pad
            if spare:
                tall.append(jnp.zeros((spare, wide), F32))
            wides.append(jnp.transpose(jnp.concatenate(tall, 0)))
        for w in range(bands):
            for i in range(0, SUB, 2):
                two = [wides[i + k][w * band : w * band + SUB] for k in range(2)]
                outs[d][w, i * SUB : (i + 2) * SUB, :] = jnp.concatenate(two, 0).astype(BF16)


def legendre_sums(steps, blocks, table, own_pairs, bands, waves, pad):
    own, degrees, lats = table.shape
    wide = -(-lats // LANES) * LANES
    out = jax.ShapeDtypeStruct((bands, SUB * SUB, LANES), BF16)
    vmem = pl.BlockSpec(memory_space=pltpu.VMEM)
    return pl.pallas_call(
        functools.partial(legendre_kernel, steps, bands, waves, pad),
        out_shape=[out] * len(steps),
        in_specs=[pl.BlockSpec(memory_space=pltpu.SMEM)] + [vmem] * (len(steps) + 1),
        scratch_shapes=[pltpu.VMEM((len(steps), pad, SUB, wide), F32)],
        compiler_params=params(40),
        name="legendre",
    )(own_pairs, *blocks, table)


def wraps(levels):
    def to_east(x):
        return pltpu.roll(x, levels, 0)

    def to_west(x):
        return pltpu.roll(x, SUB - levels, 0)

    return to_east, to_west


def from_west(values, levels):
    to_east, _ = wraps(levels)
    first = lane_index() == 0
    rolled = [pltpu.roll(x, 1, 1) for x in values]
    before = [to_east(rolled[-1])] + rolled[:-1]
    return [jnp.where(first, b, r) for b, r in zip(before, rolled)]


def from_east(values, levels):
    _, to_west = wraps(levels)
    last = lane_index() == LANES - 1
    rolled = [pltpu.roll(x, LANES - 1, 1) for x in values]
    after = rolled[1:] + [to_west(rolled[0])]
    return [jnp.where(last, a, r) for a, r in zip(after, rolled)]


def courant_kernel(lon, lat, below, above, cx, cy, ax, bx, ay, by):
    levels, band, nlon = lon.shape
    parts = SUB // levels
    rows, chunks = cx.shape[:2]
    for field, (own, out) in enumerate(((lon, cx), (lat, cy))):
        for block in range(rows // SUB):

            def chunk(v, carry, field=field, own=own, out=out, block=block):
                tiles = []
                for part in range(parts):
                    lanes = pl.ds(pl.multiple_of(part * (nlon // parts) + v * LANES, LANES), LANES)
                    if 0 < block < rows // SUB - 1:
                        for level in range(levels):
                            tiles.append(own[level, (block - 1) * SUB : block * SUB, lanes])
                    else:
                        far = below if block == 0 else above
                        for level in range(0, levels, 2):
                            first = (field * levels + level) * SUB
                            both = far[first : first + 2 * SUB, lanes].astype(F32)
                            tiles += [both[:SUB], both[SUB:]]
                turned = jnp.swapaxes(jnp.stack(tiles, 0), 0, 1)
                for t in range(SUB):
                    out[block * SUB + t, v] = turned[t]
                return carry

            lax.fori_loop(0, chunks, chunk, 0)

    def factors(t, carry):
        u = [cx[t, v] for v in range(chunks)]
        w = [cy[t, v] for v in range(chunks)]
        near = [w[v] + cy[t + 1, v] for v in range(chunks)]
        mean = [a + b for a, b in zip(near, from_west(near, levels))]
        for v in range(chunks):
            ax[t, v] = 0.5 * (jnp.abs(u[v]) - u[v] * u[v])
            bx[t, v] = 0.0625 * u[v] * mean[v]
        near = [u[v] + cx[t - 1, v] for v in range(chunks)]
        mean = [a + b for a, b in zip(near, from_east(near, levels))]
        for v in range(chunks):
            ay[t, v] = 0.5 * (jnp.abs(w[v]) - w[v] * w[v])
            by[t, v] = 0.0625 * w[v] * mean[v]
        return carry

    lax.fori_loop(1, rows - 1, factors, 0)


def courant_fields(lon, lat, below, above):
    levels, band, nlon = lon.shape
    chunks = nlon * levels // (SUB * LANES)
    out = jax.ShapeDtypeStruct((band + 2 * HALO, chunks, SUB, LANES), F32)
    return pl.pallas_call(
        courant_kernel, out_shape=[out] * 6, compiler_params=params(40), name="courant"
    )(lon, lat, below, above)


def real_transform(real, imag):
    n = len(real)
    half, quarter = n // 2, n // 4

    def weighted(terms):
        total = None
        for factor, value in terms:
            if abs(factor) < 1e-9:
                continue
            if abs(abs(factor) - 1.0) < 1e-9:
                total = (value if factor > 0 else -value) if total is None else (
                    total + value if factor > 0 else total - value
                )
            else:
                total = factor * value if total is None else total + factor * value
        return total

    def sums(odd):
        cosines, sines = [], []
        numbers = range(odd, half, 2)
        for a in range(quarter + 1):
            sign = -1.0 if a % 2 else 1.0
            angle = [2.0 * math.pi * m * a / n for m in numbers]
            cosines.append(
                weighted([(math.cos(x), combined[sign][0][m]) for x, m in zip(angle, numbers)])
            )
            sines.append(
                weighted([(math.sin(x), combined[sign][1][m]) for x, m in zip(angle, numbers)])
            )
        return cosines, sines

    def add(x, y):
        return y if x is None else x if y is None else x + y

    def negative(x):
        return None if x is None else -x

    def subtract(x, y):
        return negative(y) if x is None else x if y is None else x - y

    combined = {
        sign: [
            [part[m] + part[m + half] if sign > 0 else part[m] - part[m + half] for m in range(half)]
            for part in (real, imag)
        ]
        for sign in (1.0, -1.0)
    }
    even_cos, even_sin = sums(0)
    odd_cos, odd_sin = sums(1)
    even, odd = [None] * half, [None] * half
    for a in range(quarter + 1):
        even[a] = subtract(even_cos[a], even_sin[a])
        odd[a] = subtract(odd_cos[a], odd_sin[a])
        if 0 < a < half - a:
            even[half - a] = add(even_cos[a], even_sin[a])
            odd[half - a] = negative(add(odd_cos[a], odd_sin[a]))
    return [add(e, o) for e, o in zip(even, odd)] + [subtract(e, o) for e, o in zip(even, odd)]


def transform(arrived, order, table, lhs, mixed, inner, tiles, field, pad, levels):
    sources = arrived.shape[0]
    rows, chunks = field.shape[:2]
    pieces = rows // SUB
    group = LANES // pad
    lane = lax.broadcasted_iota(jnp.int32, (SUB * SUB, LANES), 1)
    height = levels * SUB
    for g in range(-(-sources // group)):
        members = [arrived[q].astype(F32) for q in range(g * group, min(sources, (g + 1) * group))]
        for piece in range(pieces):
            value = None
            for i, member in enumerate(members):
                shift = pad * (i - piece) % LANES
                turned = pltpu.roll(member, shift, 1) if shift else member
                value = turned if value is None else jnp.where(lane >= i * pad, turned, value)
            value = value.astype(BF16)
            for c in range(2):
                first = (c * pieces + piece) * height
                lhs[first : first + height, g * LANES : (g + 1) * LANES] = value[
                    c * height : (c + 1) * height
                ]
    half = pieces * height
    waves = order.shape[1]
    far, depth = table.shape[0], waves // table.shape[0]
    left = lax.broadcasted_iota(jnp.int32, (half, LANES), 1) < depth
    for lo in range(0, waves, NEAR):
        width = min(NEAR, waves - lo)
        got = jnp.dot(lhs[...], order[:, lo : lo + width], preferred_element_type=F32)
        for k in range(0, width, LANES):
            real, imag = got[:half, k : k + LANES], got[half:, k : k + LANES]
            m = (lo + k) // depth
            mixed[m] = jnp.where(left, real, pltpu.roll(imag, depth, 1)).astype(BF16)
            mixed[m + 1] = jnp.where(left, pltpu.roll(real, depth, 1), imag).astype(BF16)

    def mix(m, carry):
        value = mixed[m]
        inner[m] = jnp.dot(
            jnp.concatenate([value, value], 1), table[m], preferred_element_type=F32
        )
        return carry

    lax.fori_loop(0, far, mix, 0)
    parts = SUB // levels
    per_part = far // parts

    def finish(piece, carry):
        for near in range(0, NEAR, LANES):
            for level in range(levels):
                span = pl.ds(pl.multiple_of((piece * levels + level) * SUB, SUB), SUB)
                real = [inner[m, span, near : near + LANES] for m in range(far)]
                imag = [inner[m, span, NEAR + near : NEAR + near + LANES] for m in range(far)]
                for a, value in enumerate(real_transform(real, imag)):
                    tiles[a % per_part, a // per_part * levels + level] = value
            for a in range(per_part):
                turned = jnp.swapaxes(tiles[a], 0, 1)
                for t in range(SUB):
                    field[piece * SUB + t, a * (NEAR // LANES) + near // LANES] = turned[t]
        return carry

    lax.fori_loop(0, pieces, finish, 0)


def upwind_rows(t, count, old, new, cx, cy, levels):
    chunks = old.shape[1]
    to_east, to_west = wraps(levels)
    lane = lane_index()
    first, last = lane == 0, lane == LANES - 1
    rolled = [to_east(pltpu.roll(old[t + r, chunks - 1], 1, 1)) for r in range(count)]
    flux_first, flux_left, base_left = None, None, None
    for v in range(chunks + 1):
        if v < chunks:
            q = [old[t - 1 + r, v] for r in range(count + 2)]
            flux_lat = []
            for r in range(count + 1):
                speed = cy[t + r, v]
                flux_lat.append(jnp.maximum(speed, 0.0) * q[r] + jnp.minimum(speed, 0.0) * q[r + 1])
            fluxes, base = [], []
            for r in range(count):
                turned = pltpu.roll(q[r + 1], 1, 1)
                west = jnp.where(first, rolled[r], turned)
                rolled[r] = turned
                speed = cx[t + r, v]
                flux = jnp.maximum(speed, 0.0) * west + jnp.minimum(speed, 0.0) * q[r + 1]
                base.append((q[r + 1] + flux) - (flux_lat[r + 1] - flux_lat[r]))
                fluxes.append(pltpu.roll(flux, LANES - 1, 1))
            if v == 0:
                flux_first = fluxes
        else:
            fluxes = [to_west(x) for x in flux_first]
        if v > 0:
            for r in range(count):
                new[t + r, v - 1] = base_left[r] - jnp.where(last, fluxes[r], flux_left[r])
        flux_left, base_left = fluxes, base


def corrective_rows(t, count, old, new, ax, bx, ay, by, levels):
    chunks = old.shape[1]
    to_east, to_west = wraps(levels)
    lane = lane_index()
    first, last = lane == 0, lane == LANES - 1
    span = range(count + 2)

    def inverse(x):
        return pl.reciprocal(jnp.maximum(x, 1.0), approx=True)

    def flux(a, b, gradient, cross, total, step):
        speed = a * gradient - b * cross
        return speed * total - jnp.abs(speed) * step

    right = [to_east(pltpu.roll(old[t - 1 + r, chunks - 1], 1, 1)) for r in span]
    here = [old[t - 1 + r, 0] for r in span]
    left = [pltpu.roll(x, LANES - 1, 1) for x in here]
    left_first = left
    flux_first, flux_left, base_left = None, None, None
    for v in range(chunks + 1):
        if v < chunks:
            if v + 1 < chunks:
                following = [old[t - 1 + r, v + 1] for r in span]
                left_next = [pltpu.roll(x, LANES - 1, 1) for x in following]
            else:
                following, left_next = None, [to_west(x) for x in left_first]
            right_here = [pltpu.roll(x, 1, 1) for x in here]
            west = [jnp.where(first, right[r], right_here[r]) for r in span]
            east = [jnp.where(last, left_next[r], left[r]) for r in span]
            size = [jnp.abs(x) for x in here]
            size_west = [jnp.abs(x) for x in west]
            size_east = [jnp.abs(x) for x in east]
            total = [here[r] + west[r] for r in span]
            sizes = [size[r] + size_west[r] for r in span]
            apart = [east[r] - west[r] for r in span]
            sizes_apart = [size_east[r] + size_west[r] for r in span]
            flux_lat = []
            for r in range(count + 1):
                step = here[r + 1] - here[r]
                gradient = step * inverse(size[r + 1] + size[r])
                cross = (apart[r + 1] + apart[r]) * inverse(sizes_apart[r + 1] + sizes_apart[r])
                flux_lat.append(
                    flux(ay[t + r, v], by[t + r, v], gradient, cross, here[r + 1] + here[r], step)
                )
            fluxes, base = [], []
            for r in range(1, count + 1):
                step = here[r] - west[r]
                gradient = step * inverse(sizes[r])
                cross = (total[r + 1] - total[r - 1]) * inverse(sizes[r + 1] + sizes[r - 1])
                value = flux(ax[t + r - 1, v], bx[t + r - 1, v], gradient, cross, total[r], step)
                base.append((here[r] + value) - (flux_lat[r] - flux_lat[r - 1]))
                fluxes.append(pltpu.roll(value, LANES - 1, 1))
            if v == 0:
                flux_first = fluxes
            right, here, left = right_here, following, left_next
        else:
            fluxes = [to_west(x) for x in flux_first]
        if v > 0:
            for r in range(count):
                new[t + r, v - 1] = base_left[r] - jnp.where(last, fluxes[r], flux_left[r])
        flux_left, base_left = fluxes, base


def advect_kernel(
    pad, arrived, order, table, cx, cy, ax, bx, ay, by, out, lhs, mixed, inner, tiles, field, upwind
):
    levels, band, nlon = out.shape
    rows, chunks = field.shape[:2]
    transform(arrived, order, table, lhs, mixed, inner, tiles, field, pad, levels)
    outermost = lax.axis_index("wave") == 0

    def clear(where):
        @pl.when(outermost)
        def _():
            where[HALO - 1] = jnp.zeros((chunks, SUB, LANES), F32)

    def one_pass(number, carry):
        start = 2 * number + 1

        def first(i, carry):
            upwind_rows(start + 2 * i, 2, field, upwind, cx, cy, levels)
            return carry

        lax.fori_loop(0, rows // 2 - 1 - 2 * number, first, 0)
        clear(upwind)

        def second(i, carry):
            corrective_rows(start + 1 + 4 * i, 4, upwind, field, ax, bx, ay, by, levels)
            return carry

        lax.fori_loop(0, rows // 4 - 1 - number, second, 0)
        clear(field)
        return carry

    lax.fori_loop(0, PASSES, one_pass, 0)
    parts = SUB // levels
    for block in range(band // SUB):
        first = HALO + block * SUB
        for v in range(chunks):
            turned = jnp.swapaxes(field[first : first + SUB, v], 0, 1)
            for part in range(parts):
                lanes = part * (nlon // parts) + v * LANES
                for level in range(levels):
                    out[level, block * SUB : (block + 1) * SUB, lanes : lanes + LANES] = turned[
                        part * levels + level
                    ]


def advect(arrived, order, table, fields, shape, pad):
    levels, band, nlon = shape
    rows, chunks = fields[0].shape[:2]
    half = rows * levels
    far = table.shape[0]
    return pl.pallas_call(
        functools.partial(advect_kernel, pad),
        out_shape=jax.ShapeDtypeStruct(shape, F32),
        scratch_shapes=[
            pltpu.VMEM((2 * half, order.shape[0]), BF16),
            pltpu.VMEM((far, half, LANES), BF16),
            pltpu.VMEM((far, half, 2 * NEAR), F32),
            pltpu.VMEM((far * levels // SUB, SUB, SUB, LANES), F32),
            pltpu.VMEM((rows, chunks, SUB, LANES), F32),
            pltpu.VMEM((rows, chunks, SUB, LANES), F32),
        ],
        compiler_params=params(56),
        name="advect",
    )(arrived, order, table, *fields)


def mixing_table(waves, nlon):
    far = nlon // NEAR
    depth = waves // far
    number = far * np.arange(depth)[None, :, None] + np.arange(far)[:, None, None]
    angle = 2.0 * np.pi / nlon * (number * np.arange(NEAR)[None, None, :] % nlon)
    cos, sin = np.cos(angle), np.sin(angle)
    whole = np.concatenate(
        [np.concatenate([cos, sin], 2), np.concatenate([-sin, cos], 2)], 1
    ).astype(np.float32)
    high = whole.astype(ml_dtypes.bfloat16)
    low = (whole - high.astype(np.float32)).astype(ml_dtypes.bfloat16)
    return np.concatenate([high, low], 1)


def order_matrix(wave_table, sources, pad, far):
    waves = 2 * wave_table.shape[0]
    group = LANES // pad
    numbers = jnp.stack([wave_table, waves - 1 - wave_table], 1).reshape(sources, -1)
    column = numbers % far * (waves // far) + numbers // far
    extra = -sources % group
    column = jnp.pad(column, ((0, extra), (0, pad - column.shape[1])), constant_values=-1)
    column = column.reshape(-1, group * pad)
    column = jnp.pad(column, ((0, 0), (0, LANES - group * pad)), constant_values=-1).reshape(-1, 1)
    weight = jnp.where(column == 0, 1.0, 2.0).astype(BF16)
    return jnp.where(jnp.arange(waves)[None, :] == column, weight, jnp.zeros((), BF16))


def body(spectral, legendre, wave_table, courant_lon, courant_lat):
    wave_count, level_count = lax.axis_size("wave"), lax.axis_size("lev")
    wave_rank, level_rank = lax.axis_index("wave"), lax.axis_index("lev")
    levels, band, nlon = courant_lon.shape
    own = legendre.shape[0]
    waves = 2 * wave_table.shape[0]
    pad = -(-2 * own // SUB) * SUB

    up = [(i, i + 1) for i in range(wave_count - 1)]
    down = [(i + 1, i) for i in range(wave_count - 1)]
    winds = jnp.stack([courant_lon, courant_lat], 0).astype(BF16)
    upper = winds[:, :, band - HALO :].reshape(-1, nlon)
    lower = winds[:, :, :HALO].reshape(-1, nlon)

    blocks = list(pack(spectral, level_count))
    for step in range(1, level_count):
        pairs = [(i, i ^ step) for i in range(level_count)]
        blocks[step] = lax.ppermute(blocks[step], "lev", pairs)
    below = lax.ppermute(upper, "wave", up)
    above = lax.ppermute(lower, "wave", down)

    own_pairs = lax.dynamic_slice_in_dim(
        wave_table, (wave_rank * level_count + level_rank) * own, own
    )
    half = level_count // 2
    sums = []
    for steps in (tuple(range(half)), tuple(range(half, level_count))):
        sums += legendre_sums(
            steps, [blocks[s] for s in steps], legendre, own_pairs, wave_count, waves, pad
        )
    stacked = jnp.stack(sums, 1)
    stacked = jnp.take(stacked, level_rank ^ jnp.arange(level_count), axis=1)
    arrived = lax.all_to_all(
        stacked.reshape(-1, SUB * SUB, LANES), ("wave", "lev"), 0, 0, tiled=True
    )

    fields = courant_fields(courant_lon, courant_lat, below, above)
    table = jnp.asarray(mixing_table(waves, nlon))
    order = order_matrix(wave_table, wave_count * level_count, pad, nlon // NEAR)
    return advect(arrived, order, table, fields, courant_lon.shape, pad)


def solution(mesh):
    placed = (
        P(None, "lev", "wave", None),
        P(("wave", "lev"), None, None),
        P(),
        P("lev", "wave", None),
        P("lev", "wave", None),
    )
    return jax.shard_map(
        body, mesh=mesh, in_specs=placed, out_specs=P("lev", "wave", None), check_vma=False
    )
```

```python
import functools
import math

import jax
import jax.numpy as jnp
import ml_dtypes
import numpy as np
from jax import lax
from jax.experimental import pallas as pl
from jax.experimental.pallas import tpu as pltpu
from jax.sharding import PartitionSpec as P

PASSES = 4
HALO = 2 * PASSES
SUB = 8
LANES = 128
F32 = jnp.float32
BF16 = jnp.bfloat16


def params(mib):
    return pltpu.CompilerParams(vmem_limit_bytes=mib << 20)


def lane_index():
    return lax.broadcasted_iota(jnp.int32, (SUB, LANES), 1)


def pack_kernel(count, x_ref, *refs):
    outs, turned = refs[:count], refs[count]
    slots, degrees = x_ref.shape[1:]
    own = slots // count
    me = lax.axis_index("lev")

    def gather(first, rows):
        for lo in range(0, degrees, LANES):
            hi = min(lo + LANES, degrees)
            tile = jnp.stack(
                [x_ref[i, first : first + rows, lo:hi].astype(F32) for i in range(SUB)], 0
            )
            turned[first : first + rows, :, lo:hi] = jnp.swapaxes(tile, 0, 1)

    for first in range(0, slots, SUB):
        gather(first, SUB)
    for step, out in enumerate(outs):
        start = (me ^ step) * own

        def pair(i, carry, out=out, start=start):
            second = jnp.minimum(start + 2 * i + 1, slots - 1)
            both = [turned[start + 2 * i], turned[second]]
            out[i] = jnp.concatenate(both, 0).astype(BF16)
            return carry

        lax.fori_loop(0, out.shape[0], pair, 0)


def pack(spectral, count):
    parts, levels, slots, degrees = spectral.shape
    out = jax.ShapeDtypeStruct((-(-slots // count // 2), 2 * SUB, degrees), BF16)
    return pl.pallas_call(
        functools.partial(pack_kernel, count),
        out_shape=[out] * count,
        scratch_shapes=[pltpu.VMEM((slots, SUB, degrees), F32)],
        compiler_params=params(40),
        name="pack",
    )(spectral.reshape(parts * levels, slots, degrees))


def legendre_kernel(steps, bands, waves, pad, early, pairs_ref, *refs):
    count = len(steps)
    blocks, table, done = refs[:count], refs[count], refs[count + 1 : count + 1 + early]
    outs, sums = refs[count + 1 + early : -1], refs[-1]
    if early:
        me = lax.axis_index("lev")
        outs = [outs[0].at[:, me ^ step] for step in range(early + count)]
        for value, out in zip(done, outs):
            out[...] = value[...]
        outs = outs[early:]
    own, lats, degrees = table.shape
    wide = sums.shape[-1]
    band = lats // bands
    pieces = band // SUB + 2
    if wide > lats:
        sums[...] = jnp.zeros_like(sums)
    elif 2 * own < pad:
        sums[:, 2 * own :] = jnp.zeros((count, pad - 2 * own, SUB, wide), F32)

    def pair(i, carry):
        rows = jnp.concatenate([block[i] for block in blocks], 0).astype(F32)
        row = lax.broadcasted_iota(jnp.int32, rows.shape, 0) % (2 * SUB)
        degree = lax.broadcasted_iota(jnp.int32, rows.shape, 1)
        second = jnp.minimum(2 * i + 1, own - 1)
        bound = waves - jnp.where(row < SUB, pairs_ref[2 * i], pairs_ref[second])
        low = jnp.where(degree < bound, rows, 0.0)
        both = jnp.concatenate([low, rows - low], 0).astype(BF16)
        for j in range(2):
            got = lax.dot_general(
                both,
                table[second if j else 2 * i],
                (((1,), (1,)), ((), ())),
                preferred_element_type=F32,
            )
            for half in range(2):
                for d in range(count):
                    first = (half * count + d) * 2 * SUB + j * SUB
                    sums[d, 4 * i + 2 * j + half, :, :lats] = got[first : first + SUB]
        return carry

    lax.fori_loop(0, blocks[0].shape[0], pair, 0, unroll=5)
    lane = lane_index()
    nothing = jnp.zeros((SUB, LANES), F32)
    for d in range(count):
        tiles = [
            [jnp.swapaxes(sums[d, 8 * g : 8 * g + 8, :, k : k + LANES], 0, 1) for k in range(0, wide, LANES)]
            for g in range(pad // SUB)
        ]
        stood = []
        for i in range(SUB):
            once = [jnp.concatenate([tile[i] for tile in row], 1) for row in tiles]
            spare = (LANES - pieces * pad) // SUB
            tall = once * pieces + [jnp.zeros((SUB, wide), F32)] * spare
            stood.append(jnp.transpose(jnp.concatenate(tall, 0)))
        for w in range(bands):
            for i in range(0, SUB, 2):
                two = []
                for value in stood[i : i + 2]:
                    tile = nothing
                    for piece in reversed(range(pieces)):
                        first = w * band + (piece - 1) * SUB
                        there = value[first : first + SUB] if 0 <= first < lats else nothing
                        tile = there if piece == pieces - 1 else jnp.where(
                            lane < (piece + 1) * pad, there, tile
                        )
                    two.append(tile)
                outs[d][w, i * SUB : (i + 2) * SUB, :] = jnp.concatenate(two, 0).astype(BF16)


def legendre_sums(steps, blocks, table, own_pairs, bands, waves, pad, done=()):
    own, lats, degrees = table.shape
    wide = -(-lats // LANES) * LANES
    outs = [jax.ShapeDtypeStruct((bands, SUB * SUB, LANES), BF16)] * len(steps)
    if done:
        outs = jax.ShapeDtypeStruct((bands, len(done) + len(steps), SUB * SUB, LANES), BF16)
    vmem = pl.BlockSpec(memory_space=pltpu.VMEM)
    return pl.pallas_call(
        functools.partial(legendre_kernel, steps, bands, waves, pad, len(done)),
        out_shape=outs,
        in_specs=[pl.BlockSpec(memory_space=pltpu.SMEM)] + [vmem] * (len(steps) + 1 + len(done)),
        scratch_shapes=[pltpu.VMEM((len(steps), pad, SUB, wide), F32)],
        compiler_params=params(40),
        name="legendre",
    )(own_pairs, *blocks, table, *done)


def west_of_first(last_chunk, levels):
    turned = pltpu.roll(last_chunk, 1, 1)
    return jnp.where(lane_index() == 0, pltpu.roll(turned, levels, 0), turned)


def east_of_last(first_chunk, levels):
    turned = pltpu.roll(first_chunk, LANES - 1, 1)
    return jnp.where(lane_index() == LANES - 1, pltpu.roll(turned, SUB - levels, 0), turned)


def courant_kernel(lon, lat, below, above, far_fields, fields, turned, sems):
    cx, cy, ax, bx, ay, by = [fields.at[i] for i in range(6)]
    levels, band, nlon = lon.shape
    parts = SUB // levels
    rows, chunks = cx.shape[:2]
    span = nlon // parts
    for block in range(rows // SUB):

        def stand(n, carry, block=block):
            tiles = []
            for field, own in enumerate((lon, lat)):
                for part in range(parts):
                    lanes = pl.ds(pl.multiple_of(part * span + n * LANES, LANES), LANES)
                    if 0 < block < rows // SUB - 1:
                        for level in range(levels):
                            tiles.append(own[level, (block - 1) * SUB : block * SUB, lanes])
                    else:
                        far = below if block == 0 else above
                        first = field * levels * SUB
                        tiles.append(far[first : first + levels * SUB, lanes].astype(F32))
            start = pl.multiple_of(n * LANES, LANES)
            turned[pl.ds(start, LANES), :] = jnp.transpose(jnp.concatenate(tiles, 0))
            return carry

        def lie(v, carry, block=block):
            value = jnp.transpose(turned[pl.ds(v, LANES, stride=chunks), :])
            for field, out in enumerate((cx, cy)):
                both = value[field * SUB * SUB : (field + 1) * SUB * SUB]
                both = jnp.swapaxes(both.reshape(SUB, SUB, LANES), 0, 1)
                for t in range(SUB):
                    out[block * SUB + t, v] = both[t]
            return carry

        lax.fori_loop(0, span // LANES, stand, 0, unroll=2)
        lax.fori_loop(0, chunks, lie, 0, unroll=2)

    copies = [pltpu.make_async_copy(fields.at[i], far_fields.at[i], sems.at[i]) for i in range(6)]
    for copy in copies[:2]:
        copy.start()
    for ref in (ax, bx, ay, by):
        for t in (0, rows - 1):
            ref[t] = jnp.zeros(ref.shape[1:], F32)

    def factors(t, carry):
        u = [cx[t, v] for v in range(chunks)]
        w = [cy[t, v] for v in range(chunks)]
        near = [w[v] + cy[t + 1, v] for v in range(chunks)]
        west = [west_of_first(near[-1], levels)] + near[:-1]
        for v in range(chunks):
            ax[t, v] = 0.5 * (jnp.abs(u[v]) - u[v] * u[v])
            bx[t, v] = 0.0625 * u[v] * (near[v] + west[v])
        near = [u[v] + cx[t - 1, v] for v in range(chunks)]
        east = near[1:] + [east_of_last(near[0], levels)]
        for v in range(chunks):
            ay[t, v] = 0.5 * (jnp.abs(w[v]) - w[v] * w[v])
            by[t, v] = 0.0625 * w[v] * (near[v] + east[v])
        return carry

    lax.fori_loop(1, rows - 1, factors, 0)
    for copy in copies[2:]:
        copy.start()
    for copy in copies:
        copy.wait()


def courant_fields(lon, lat, below, above):
    levels, band, nlon = lon.shape
    parts = SUB // levels
    chunks = nlon // (parts * LANES)
    shape = (6, band + 2 * HALO, chunks, SUB, LANES)
    return pl.pallas_call(
        courant_kernel,
        out_shape=pltpu.HBM(shape, F32),
        out_specs=pl.BlockSpec(memory_space=pltpu.HBM),
        scratch_shapes=[
            pltpu.VMEM(shape, F32),
            pltpu.VMEM((nlon // parts, LANES), F32),
            pltpu.SemaphoreType.DMA((6,)),
        ],
        compiler_params=params(28),
        cost_estimate=pl.CostEstimate(
            flops=20_000_000_000, bytes_accessed=20_000_000, transcendentals=0
        ),
        name="courant",
    )(lon, lat, below, above)


def spread(real, imag, count):
    def weighted(function, v, values, parity):
        total = None
        for m in range(parity, len(values), 2):
            factor = function(2.0 * math.pi * (m * v % count) / count)
            if abs(factor) > 1e-9:
                term = values[m] if abs(factor - 1.0) < 1e-9 else factor * values[m]
                total = term if total is None else total + term
        return total

    def add(x, y):
        return y if x is None else x if y is None else x + y

    def subtract(x, y):
        return x if y is None else -y if x is None else x - y

    half = count // 2
    out = [None] * count
    for v in range(half // 2 + 1):
        sums = [
            [weighted(function, v, values, parity) for parity in range(2)]
            for function, values in (
                (math.cos, real),
                (math.sin, imag),
                (math.cos, imag),
                (math.sin, real),
            )
        ]
        (p0, p1), (q0, q1), (r0, r1), (u0, u1) = sums
        found = [(v, add(p0, p1), add(q0, q1), add(r0, r1), add(u0, u1))]
        if v < half - v:
            found.append(
                (half - v, subtract(p0, p1), subtract(q1, q0), subtract(r0, r1), subtract(u1, u0))
            )
        for w, p, q, r, u in found:
            out[w] = (subtract(p, q), add(r, u))
            if 0 < w < half:
                out[count - w] = (add(p, q), subtract(r, u))
    return out


def transform(
    arrived, order, order_copy, twist, table, lhs, mixed, terms, field, pad, levels
):
    sources = arrived.shape[0]
    rows, chunks = field.shape[:2]
    pieces = rows // SUB
    group = LANES // pad
    lane = lax.broadcasted_iota(jnp.int32, (SUB * SUB, LANES), 1)
    height = levels * SUB
    for g in range(-(-sources // group)):
        members = [arrived[q].astype(F32) for q in range(g * group, min(sources, (g + 1) * group))]
        for piece in range(pieces):
            value = None
            for i, member in enumerate(members):
                shift = pad * (i - piece) % LANES
                turned = pltpu.roll(member, shift, 1) if shift else member
                value = turned if value is None else jnp.where(lane >= i * pad, turned, value)
            value = value.astype(BF16)
            for c in range(2):
                first = (c * pieces + piece) * height
                lhs[first : first + height, g * LANES : (g + 1) * LANES] = value[
                    c * height : (c + 1) * height
                ]
    half = pieces * height
    near = table.shape[1]
    depth = mixed.shape[0]
    order_copy.wait()
    for m in range(depth):
        mixed[m] = jnp.dot(
            lhs[...], order[:, m * near : (m + 1) * near], preferred_element_type=F32
        )

    def vary(i, carry):
        span = pl.ds(pl.multiple_of(i * 2 * SUB, 2 * SUB), 2 * SUB)
        other = pl.ds(pl.multiple_of(half + i * 2 * SUB, 2 * SUB), 2 * SUB)
        for lo in range(0, near, LANES):
            lanes = slice(lo, lo + LANES)
            real = [mixed[m, span, lanes] for m in range(depth)]
            imag = [mixed[m, other, lanes] for m in range(depth)]
            for v, (x, y) in enumerate(spread(real, imag, chunks)):
                if v:
                    cos, sin = twist[2 * v : 2 * v + 1, lanes], twist[2 * v + 1 : 2 * v + 2, lanes]
                    x, y = x * cos - y * sin, x * sin + y * cos
                for c, value in enumerate((x, y)):
                    high = value.astype(BF16)
                    low = (value - high.astype(F32)).astype(BF16)
                    terms[v, span, c * near + lo : c * near + lo + LANES] = high
                    terms[v, span, (2 + c) * near + lo : (2 + c) * near + lo + LANES] = low
        return carry

    lax.fori_loop(0, half // (2 * SUB), vary, 0)
    parts = SUB // levels

    group = chunks // 2

    def finish(i, carry):
        both = terms[pl.ds(i * group, group)].reshape(group * half, 4 * near)
        high, low = both[:, : 2 * near], both[:, 2 * near :]
        value = jnp.dot(high, table[: 2 * near], preferred_element_type=F32)
        value += jnp.dot(low, table[: 2 * near], preferred_element_type=F32)
        value += jnp.dot(high, table[2 * near :], preferred_element_type=F32)
        for v in range(group):
            for piece in range(pieces):
                tiles = []
                for part in range(parts):
                    for level in range(levels):
                        first = v * half + (piece * levels + level) * SUB
                        lanes = slice(part * LANES, (part + 1) * LANES)
                        tiles.append(value[first : first + SUB, lanes])
                turned = jnp.swapaxes(jnp.stack(tiles, 0), 0, 1)
                for t in range(SUB):
                    field[piece * SUB + t, i * group + v] = turned[t]
        return carry

    lax.fori_loop(0, chunks // group, finish, 0)


def upwind_rows(t, count, old, new, cx, cy, levels):
    chunks = old.shape[1]
    west = [west_of_first(old[t + r, chunks - 1], levels) for r in range(count)]
    first, base = None, None
    for v in range(chunks + 1):
        if v < chunks:
            q = [old[t - 1 + r, v] for r in range(count + 2)]
            flux_lat, flux_lon = [], []
            for r in range(count + 1):
                speed = cy[t + r, v]
                flux_lat.append(jnp.maximum(speed, 0.0) * q[r] + jnp.minimum(speed, 0.0) * q[r + 1])
            for r in range(count):
                speed = cx[t + r, v]
                flux_lon.append(
                    jnp.maximum(speed, 0.0) * west[r] + jnp.minimum(speed, 0.0) * q[r + 1]
                )
            west = q[1 : count + 1]
            first = flux_lon if v == 0 else first
        else:
            flux_lon = [east_of_last(x, levels) for x in first]
        for r in range(count):
            if v > 0:
                new[t + r, v - 1] = base[r] - flux_lon[r]
        if v < chunks:
            base = [q[r + 1] + flux_lon[r] - (flux_lat[r + 1] - flux_lat[r]) for r in range(count)]


def corrective_rows(t, count, old, new, ax, bx, ay, by, levels):
    chunks = old.shape[1]
    span = range(count + 2)

    def inverse(x):
        return pl.reciprocal(jnp.maximum(x, 1.0), approx=True)

    def flux(a, b, gradient, cross, total, step):
        speed = a * gradient - b * cross
        return speed * total - jnp.abs(speed) * step

    here = [old[t - 1 + r, 0] for r in span]
    start = here
    west = [west_of_first(old[t - 1 + r, chunks - 1], levels) for r in span]
    size, size_west = [jnp.abs(x) for x in here], [jnp.abs(x) for x in west]
    first, base = None, None
    for v in range(chunks + 1):
        if v < chunks:
            if v + 1 < chunks:
                east = [old[t - 1 + r, v + 1] for r in span]
            else:
                east = [east_of_last(x, levels) for x in start]
            size_east = [jnp.abs(x) for x in east]
            flux_lat, flux_lon = [], []
            apart = [east[r] - west[r] for r in span]
            sizes_apart = [size_east[r] + size_west[r] for r in span]
            for r in range(count + 1):
                step = here[r + 1] - here[r]
                gradient = step * inverse(size[r + 1] + size[r])
                cross = (apart[r + 1] + apart[r]) * inverse(sizes_apart[r + 1] + sizes_apart[r])
                flux_lat.append(
                    flux(ay[t + r, v], by[t + r, v], gradient, cross, here[r + 1] + here[r], step)
                )
            total = [here[r] + west[r] for r in span]
            sizes = [size[r] + size_west[r] for r in span]
            for r in range(1, count + 1):
                step = here[r] - west[r]
                gradient = step * inverse(sizes[r])
                cross = (total[r + 1] - total[r - 1]) * inverse(sizes[r + 1] + sizes[r - 1])
                flux_lon.append(
                    flux(ax[t + r - 1, v], bx[t + r - 1, v], gradient, cross, total[r], step)
                )
            first = flux_lon if v == 0 else first
        else:
            flux_lon = [east_of_last(x, levels) for x in first]
        for r in range(count):
            if v > 0:
                new[t + r, v - 1] = base[r] - flux_lon[r]
        if v < chunks:
            base = [
                here[r + 1] + flux_lon[r] - (flux_lat[r + 1] - flux_lat[r]) for r in range(count)
            ]
            west, here, size_west, size = here, east, size, size_east


def advect_kernel(pad, arrived, far_order, twist, table, *refs):
    far_fields, out, fields, order, lhs, mixed, terms, field, upwind, turned, sems = refs
    cx, cy, ax, bx, ay, by = [fields.at[i] for i in range(6)]
    levels, band, nlon = out.shape
    rows, chunks = field.shape[:2]
    copies = [
        pltpu.make_async_copy(far_order, order, sems.at[0]),
        pltpu.make_async_copy(far_fields, fields, sems.at[1]),
    ]
    for copy in copies:
        copy.start()
    transform(
        arrived, order, copies[0], twist, table, lhs, mixed, terms, field, pad, levels
    )
    copies[1].wait()
    outermost = lax.axis_index("wave") == 0

    def clear(where):
        @pl.when(outermost)
        def _():
            where[HALO - 1] = jnp.zeros((chunks, SUB, LANES), F32)

    def one_pass(number, carry):
        start = 2 * number + 1

        def first(i, carry):
            upwind_rows(start + 2 * i, 2, field, upwind, cx, cy, levels)
            return carry

        lax.fori_loop(0, rows // 2 - 1 - 2 * number, first, 0)
        clear(upwind)

        def second(i, carry):
            corrective_rows(start + 1 + 4 * i, 4, upwind, field, ax, bx, ay, by, levels)
            return carry

        lax.fori_loop(0, rows // 4 - 1 - number, second, 0)
        clear(field)
        return carry

    lax.fori_loop(0, PASSES, one_pass, 0)
    span = nlon * levels // SUB
    for block in range(band // SUB):
        first = HALO + block * SUB

        def stand(v, carry, first=first):
            value = jnp.swapaxes(field[pl.ds(first, SUB), v], 0, 1).reshape(SUB * SUB, LANES)
            value = jnp.transpose(jnp.concatenate([value, value], 0))
            turned[pl.ds(v, LANES, stride=chunks), :] = value
            return carry

        lax.fori_loop(0, chunks, stand, 0, unroll=2)
        for n in range(span // LANES):
            value = jnp.transpose(turned[n * LANES : (n + 1) * LANES, :])
            for i in range(SUB):
                lanes = i // levels * span + n * LANES
                out[i % levels, block * SUB : (block + 1) * SUB, lanes : lanes + LANES] = value[
                    i * SUB : (i + 1) * SUB
                ]


def advect(arrived, order, twist, table, fields, shape, pad):
    levels, band, nlon = shape
    rows, chunks = fields.shape[1:3]
    half = rows * levels
    near = table.shape[1]
    order, fields = (pltpu.with_memory_space_constraint(x, pltpu.HBM) for x in (order, fields))
    vmem, far = pl.BlockSpec(memory_space=pltpu.VMEM), pl.BlockSpec(memory_space=pltpu.HBM)
    return pl.pallas_call(
        functools.partial(advect_kernel, pad),
        out_shape=jax.ShapeDtypeStruct(shape, F32),
        in_specs=[vmem, far, vmem, vmem, far],
        scratch_shapes=[
            pltpu.VMEM(fields.shape, F32),
            pltpu.VMEM(order.shape, BF16),
            pltpu.VMEM((2 * half, order.shape[0]), BF16),
            pltpu.VMEM((order.shape[1] // near, 2 * half, near), F32),
            pltpu.VMEM((chunks, half, 4 * near), BF16),
            pltpu.VMEM((rows, chunks, SUB, LANES), F32),
            pltpu.VMEM((rows, chunks, SUB, LANES), F32),
            pltpu.VMEM((nlon * levels // SUB, LANES), F32),
            pltpu.SemaphoreType.DMA((2,)),
        ],
        compiler_params=params(40),
        name="advect",
    )(arrived, order, twist, table, fields)


def fourier_tables(nlon, near):
    chunks = nlon // near
    f = np.arange(near)
    angle = 2.0 * np.pi / nlon * (np.arange(chunks)[:, None] * f[None, :] % nlon)
    twist = np.stack([np.cos(angle), np.sin(angle)], 1).reshape(2 * chunks, near)
    angle = 2.0 * np.pi / near * (f[:, None] * f[None, :] % near)
    whole = np.concatenate([np.cos(angle), -np.sin(angle)], 0).astype(np.float32)
    high = whole.astype(ml_dtypes.bfloat16)
    low = (whole - high.astype(np.float32)).astype(ml_dtypes.bfloat16)
    return twist.astype(np.float32), np.concatenate([high, low], 0)


def order_matrix(wave_table, sources, pad):
    waves = 2 * wave_table.shape[0]
    group = LANES // pad
    numbers = jnp.stack([wave_table, waves - 1 - wave_table], 1).reshape(sources, -1)
    extra = -sources % group
    column = jnp.pad(numbers, ((0, extra), (0, pad - numbers.shape[1])), constant_values=-1)
    column = column.reshape(-1, group * pad)
    column = jnp.pad(column, ((0, 0), (0, LANES - group * pad)), constant_values=-1).reshape(-1, 1)
    weight = jnp.where(column == 0, 1.0, 2.0).astype(BF16)
    return jnp.where(jnp.arange(waves)[None, :] == column, weight, jnp.zeros((), BF16))


def body(spectral, legendre, wave_table, courant_lon, courant_lat):
    wave_count, level_count = lax.axis_size("wave"), lax.axis_size("lev")
    wave_rank, level_rank = lax.axis_index("wave"), lax.axis_index("lev")
    levels, band, nlon = courant_lon.shape
    own = legendre.shape[0]
    waves = 2 * wave_table.shape[0]
    pad = -(-2 * own // SUB) * SUB

    up = [(i, i + 1) for i in range(wave_count - 1)]
    down = [(i + 1, i) for i in range(wave_count - 1)]
    blocks = list(pack(spectral, level_count))
    blocks, courant_lon, courant_lat = lax.optimization_barrier(
        (blocks, courant_lon, courant_lat)
    )
    for step in range(1, level_count):
        pairs = [(i, i ^ step) for i in range(level_count)]
        blocks[step] = lax.ppermute(blocks[step], "lev", pairs)
    winds = jnp.stack([courant_lon, courant_lat], 0).astype(BF16)
    upper = winds[:, :, band - HALO :].reshape(-1, nlon)
    lower = winds[:, :, :HALO].reshape(-1, nlon)
    below = lax.ppermute(upper, "wave", up)
    above = lax.ppermute(lower, "wave", down)

    own_pairs = lax.dynamic_slice_in_dim(
        wave_table, (wave_rank * level_count + level_rank) * own, own
    )
    turned = jnp.swapaxes(legendre, 1, 2)
    half = level_count // 2
    given = (turned, own_pairs, wave_count, waves, pad)
    early = legendre_sums(range(half), blocks[:half], *given)
    order = order_matrix(wave_table, wave_count * level_count, pad)
    early, order = lax.optimization_barrier((tuple(early), order))
    stacked = legendre_sums(range(half, level_count), blocks[half:], *given, done=early)
    arrived = lax.all_to_all(
        stacked.reshape(-1, SUB * SUB, LANES), ("wave", "lev"), 0, 0, tiled=True
    )

    fields = courant_fields(courant_lon, courant_lat, below, above)
    twist, table = fourier_tables(nlon, SUB // levels * LANES)
    return advect(
        arrived, order, jnp.asarray(twist), jnp.asarray(table), fields, courant_lon.shape, pad
    )


def solution(mesh):
    placed = (
        P(None, "lev", "wave", None),
        P(("wave", "lev"), None, None),
        P(),
        P("lev", "wave", None),
        P("lev", "wave", None),
    )
    return jax.shard_map(
        body, mesh=mesh, in_specs=placed, out_specs=P("lev", "wave", None), check_vma=False
    )
```

```python
import functools
import math

import jax
import jax.numpy as jnp
import ml_dtypes
import numpy as np
from jax import lax
from jax.experimental import pallas as pl
from jax.experimental.pallas import tpu as pltpu
from jax.sharding import PartitionSpec as P

PASSES = 4
HALO = 2 * PASSES
SUB = 8
LANES = 128
F32 = jnp.float32
BF16 = jnp.bfloat16


def params(mib):
    return pltpu.CompilerParams(vmem_limit_bytes=mib << 20)


def lane_index():
    return lax.broadcasted_iota(jnp.int32, (SUB, LANES), 1)


def pack_kernel(count, steps, x_ref, *refs):
    turned = refs[-1]
    degrees = x_ref.shape[2]
    own = turned.shape[0] // (count // 2)
    pairs = -(-own // 2)
    whole = degrees // LANES
    me = lax.axis_index("lev")
    there = (me ^ steps[0]) // (count // 2)
    for part in range(2):
        start = part * turned.shape[0]
        first = start // SUB * SUB

        @pl.when(there == part)
        def _(start=start, first=first):
            for group in range(first, start + turned.shape[0], SUB):
                for lo in range(0, degrees, LANES):
                    hi = min(lo + LANES, degrees)
                    tile = [x_ref[i, group : group + SUB, lo:hi].astype(F32) for i in range(SUB)]
                    tile = jnp.swapaxes(jnp.stack(tile, 0), 0, 1)
                    skip = max(start - group, 0)
                    keep = min(start + turned.shape[0] - group, SUB)
                    at = group + skip - start
                    turned[at : at + keep - skip, :, lo:hi] = tile[skip:keep]

    lane = lax.broadcasted_iota(jnp.int32, (2 * SUB, LANES), 1)
    for step, out in zip(steps, refs):
        start = (me ^ step) % (count // 2) * own

        def two(i, start=start):
            return start + 2 * i, start + jnp.minimum(2 * i + 1, own - 1)

        def pair(i, carry, out=out, two=two):
            for n in range(whole):
                both = [turned[slot, :, n * LANES : (n + 1) * LANES] for slot in two(i)]
                row = pl.multiple_of((i * whole + n) * 2 * SUB, 2 * SUB)
                out[pl.ds(row, 2 * SUB), :] = jnp.concatenate(both, 0).astype(BF16)
            return carry

        lax.fori_loop(0, pairs, pair, 0)
        rest = jnp.zeros((2 * SUB, LANES), F32)
        for i in range(pairs):
            last = [turned[slot, :, whole * LANES :] for slot in two(i)]
            rest = jnp.where(lane == i, jnp.concatenate(last, 0), rest)
        out[pairs * whole * 2 * SUB :, :] = rest.astype(BF16)


def pack(spectral, steps, count):
    levels, slots, degrees = spectral.shape
    pairs = -(-slots // count // 2)
    out = jax.ShapeDtypeStruct(((pairs * (degrees // LANES) + 1) * 2 * SUB, LANES), BF16)
    spectral = jnp.pad(spectral, ((0, 0), (0, -slots % (2 * SUB)), (0, 0)))
    return pl.pallas_call(
        functools.partial(pack_kernel, count, steps),
        out_shape=[out] * len(steps),
        scratch_shapes=[pltpu.VMEM((slots // 2, SUB, degrees), F32)],
        compiler_params=params(40),
        name="pack",
    )(spectral)


def legendre_kernel(steps, bands, waves, pad, early, pairs_ref, *refs):
    count = len(steps)
    blocks, table, done = refs[:count], refs[count], refs[count + 1 : count + 1 + early]
    outs, sums = refs[count + 1 + early : -1], refs[-1]
    if early:
        me = lax.axis_index("lev")
        outs = [outs[0].at[:, me ^ step] for step in range(early + count)]
        for value, out in zip(done, outs):
            out[...] = value[...]
        outs = outs[early:]
    own, lats, degrees = table.shape
    whole = degrees // LANES
    wide = sums.shape[-1]
    band = lats // bands
    pieces = band // SUB + 2
    if wide > lats:
        sums[...] = jnp.zeros_like(sums)
    elif 2 * own < pad:
        sums[:, 2 * own :] = jnp.zeros((count, pad - 2 * own, SUB, wide), F32)

    def pair(i, carry):
        rows = []
        for block in blocks:
            parts = []
            for n in range(whole):
                first = pl.multiple_of((i * whole + n) * 2 * SUB, 2 * SUB)
                parts.append(block[pl.ds(first, 2 * SUB), :].astype(F32))
            rest = block[block.shape[0] - 2 * SUB :, :].astype(F32)
            parts.append(pltpu.roll(rest, (LANES - i) % LANES, 1)[:, : degrees - whole * LANES])
            rows.append(jnp.concatenate(parts, 1))
        rows = jnp.concatenate(rows, 0)
        row = lax.broadcasted_iota(jnp.int32, rows.shape, 0) % (2 * SUB)
        degree = lax.broadcasted_iota(jnp.int32, rows.shape, 1)
        second = jnp.minimum(2 * i + 1, own - 1)
        bound = waves - jnp.where(row < SUB, pairs_ref[2 * i], pairs_ref[second])
        low = jnp.where(degree < bound, rows, 0.0)
        both = jnp.concatenate([low, rows - low], 0).astype(BF16)
        for j in range(2):
            got = lax.dot_general(
                both,
                table[second if j else 2 * i],
                (((1,), (1,)), ((), ())),
                preferred_element_type=F32,
            )
            for half in range(2):
                for d in range(count):
                    first = (half * count + d) * 2 * SUB + j * SUB
                    sums[d, 4 * i + 2 * j + half, :, :lats] = got[first : first + SUB]
        return carry

    lax.fori_loop(0, -(-own // 2), pair, 0, unroll=5)
    lane = lane_index()
    nothing = jnp.zeros((SUB, LANES), F32)
    for d in range(count):
        tiles = [
            [jnp.swapaxes(sums[d, 8 * g : 8 * g + 8, :, k : k + LANES], 0, 1) for k in range(0, wide, LANES)]
            for g in range(pad // SUB)
        ]
        stood = []
        for i in range(SUB):
            once = [jnp.concatenate([tile[i] for tile in row], 1) for row in tiles]
            spare = (LANES - pieces * pad) // SUB
            tall = once * pieces + [jnp.zeros((SUB, wide), F32)] * spare
            stood.append(jnp.transpose(jnp.concatenate(tall, 0)))
        for w in range(bands):
            for i in range(0, SUB, 2):
                two = []
                for value in stood[i : i + 2]:
                    tile = nothing
                    for piece in reversed(range(pieces)):
                        first = w * band + (piece - 1) * SUB
                        there = value[first : first + SUB] if 0 <= first < lats else nothing
                        tile = there if piece == pieces - 1 else jnp.where(
                            lane < (piece + 1) * pad, there, tile
                        )
                    two.append(tile)
                outs[d][w, i * SUB : (i + 2) * SUB, :] = jnp.concatenate(two, 0).astype(BF16)


def legendre_sums(steps, blocks, table, own_pairs, bands, waves, pad, done=()):
    own, lats, degrees = table.shape
    wide = -(-lats // LANES) * LANES
    outs = [jax.ShapeDtypeStruct((bands, SUB * SUB, LANES), BF16)] * len(steps)
    if done:
        outs = jax.ShapeDtypeStruct((bands, len(done) + len(steps), SUB * SUB, LANES), BF16)
    vmem = pl.BlockSpec(memory_space=pltpu.VMEM)
    return pl.pallas_call(
        functools.partial(legendre_kernel, steps, bands, waves, pad, len(done)),
        out_shape=outs,
        in_specs=[pl.BlockSpec(memory_space=pltpu.SMEM)] + [vmem] * (len(steps) + 1 + len(done)),
        scratch_shapes=[pltpu.VMEM((len(steps), pad, SUB, wide), F32)],
        compiler_params=params(40),
        name="legendre",
    )(own_pairs, *blocks, table, *done)


def west_of_first(last_chunk, levels):
    turned = pltpu.roll(last_chunk, 1, 1)
    return jnp.where(lane_index() == 0, pltpu.roll(turned, levels, 0), turned)


def east_of_last(first_chunk, levels):
    turned = pltpu.roll(first_chunk, LANES - 1, 1)
    return jnp.where(lane_index() == LANES - 1, pltpu.roll(turned, SUB - levels, 0), turned)


def halo_kernel(lon, lat, *refs):
    levels, band = lon.shape[:2]
    for halo, start in zip(refs, (0, band - HALO)):
        for field, wind in enumerate((lon, lat)):
            for level in range(0, levels, 2):
                both = [wind[level + k, start : start + HALO, :] for k in range(2)]
                row = (field * levels + level) * HALO
                halo[row : row + 2 * HALO, :] = jnp.concatenate(both, 0).astype(BF16)


def halos(lon, lat):
    levels, band, nlon = lon.shape
    halo = jax.ShapeDtypeStruct((2 * levels * HALO, nlon), BF16)
    made = pl.pallas_call(
        halo_kernel,
        out_shape=[halo] * (1 if band == HALO else 2),
        compiler_params=params(12),
        name="halos",
    )(lon, lat)
    return made[0], made[-1]


def turn(tiles_of, rows, start, turned):
    chunks = rows.shape[2]

    def stand(n, carry):
        first = pl.multiple_of(n * LANES, LANES)
        turned[pl.ds(first, LANES), :] = jnp.transpose(jnp.concatenate(tiles_of(n), 0))
        return carry

    def lie(v, carry):
        value = jnp.transpose(turned[pl.ds(v, LANES, stride=chunks), :])
        for field in range(2):
            both = value[field * SUB * SUB : (field + 1) * SUB * SUB]
            both = jnp.swapaxes(both.reshape(SUB, SUB, LANES), 0, 1)
            for t in range(SUB):
                rows[field, start + t, v] = both[t]
        return carry

    lax.fori_loop(0, turned.shape[0] // LANES, stand, 0, unroll=4)
    lax.fori_loop(0, chunks, lie, 0, unroll=4)


def lanes_of(part, n, span):
    return pl.ds(pl.multiple_of(part * span + n * LANES, LANES), LANES)


def own_courant_kernel(lon, lat, own, rows, turned, sem):
    levels, band, _ = lon.shape
    for start in range(0, band, SUB):

        def tiles_of(n, start=start):
            return [
                wind[level, start : start + SUB, lanes_of(part, n, turned.shape[0])]
                for wind in (lon, lat)
                for part in range(SUB // levels)
                for level in range(levels)
            ]

        turn(tiles_of, rows, start, turned)
    copy = pltpu.make_async_copy(rows, own, sem)
    copy.start()
    copy.wait()


def own_courant(lon, lat):
    levels, band, nlon = lon.shape
    parts = SUB // levels
    shape = (2, band, nlon // (parts * LANES), SUB, LANES)
    return pl.pallas_call(
        own_courant_kernel,
        out_shape=pltpu.HBM(shape, F32),
        out_specs=pl.BlockSpec(memory_space=pltpu.HBM),
        scratch_shapes=[
            pltpu.VMEM(shape, F32),
            pltpu.VMEM((nlon // parts, LANES), F32),
            pltpu.SemaphoreType.DMA,
        ],
        compiler_params=params(16),
        name="own_courant",
    )(lon, lat)


def factor_kernel(levels, side, own, *refs):
    far_out, fields, sems = refs[1:4] if side else refs
    cx, cy, ax, bx, ay, by = [fields.at[i] for i in range(6)]
    rows, chunks = fields.shape[1:3]
    band = own.shape[1]
    if side:
        start, at = (0, HALO) if side < 0 else (band - 2, 0)
        source, target = own.at[:, pl.ds(start, 2)], fields.at[pl.ds(0, 2), pl.ds(at, 2)]
    else:
        source, target = own, fields.at[pl.ds(0, 2)]
    copy = pltpu.make_async_copy(source, target, sems.at[0])
    copy.start()
    if side:
        received, turned = refs[0], refs[-1]

        def tiles_of(n):
            height = levels * SUB
            return [
                received[wind * height : (wind + 1) * height, lanes_of(part, n, turned.shape[0])].astype(F32)
                for wind in range(2)
                for part in range(SUB // levels)
            ]

        turn(tiles_of, fields, 0 if side < 0 else 2, turned)
    copy.wait()
    low = 0 if side < 0 else 1
    height = far_out.shape[1]
    copies = [
        pltpu.make_async_copy(
            fields.at[pl.ds(i, count), pl.ds(low, height)],
            far_out.at[pl.ds(i, count)],
            sems.at[1 + k],
        )
        for k, (i, count) in enumerate(((0, 2), (2, 4)))
    ]
    copies[0].start()
    if side:
        for i in range(2, 6):
            fields[i, 0 if side < 0 else rows - 1] = jnp.zeros((chunks, SUB, LANES), F32)

    def factors(t, carry):
        u = [cx[t, v] for v in range(chunks)]
        w = [cy[t, v] for v in range(chunks)]
        near = [w[v] + cy[t + 1, v] for v in range(chunks)]
        west = [west_of_first(near[-1], levels)] + near[:-1]
        for v in range(chunks):
            ax[t, v] = 0.5 * (jnp.abs(u[v]) - u[v] * u[v])
            bx[t, v] = 0.0625 * u[v] * (near[v] + west[v])
        near = [u[v] + cx[t - 1, v] for v in range(chunks)]
        east = near[1:] + [east_of_last(near[0], levels)]
        for v in range(chunks):
            ay[t, v] = 0.5 * (jnp.abs(w[v]) - w[v] * w[v])
            by[t, v] = 0.0625 * w[v] * (near[v] + east[v])
        return carry

    lax.fori_loop(1, rows - 1, factors, 0)
    copies[1].start()
    for copy in copies:
        copy.wait()


def factor_rows(own, received, side, levels):
    _, band, chunks, _, _ = own.shape
    rows = HALO + 2 if side else band
    out = HALO + 1 if side else band - 2
    vmem, far = pl.BlockSpec(memory_space=pltpu.VMEM), pl.BlockSpec(memory_space=pltpu.HBM)
    extra = (received,) if side else ()
    return pl.pallas_call(
        functools.partial(factor_kernel, levels, side),
        out_shape=pltpu.HBM((6, out, chunks, SUB, LANES), F32),
        in_specs=[far] + [vmem] * len(extra),
        out_specs=far,
        scratch_shapes=[
            pltpu.VMEM((6, rows, chunks, SUB, LANES), F32),
            pltpu.SemaphoreType.DMA((3,)),
        ]
        + [pltpu.VMEM((chunks * LANES, LANES), F32)] * len(extra),
        compiler_params=params(16),
        cost_estimate=pl.CostEstimate(
            flops=30_000_000_000 if side > 0 else 1_000_000_000,
            bytes_accessed=8_000_000,
            transcendentals=0,
        ),
        name="factors",
    )(pltpu.with_memory_space_constraint(own, pltpu.HBM), *extra)


def spread(real, imag, count):
    def weighted(function, v, values, parity):
        total = None
        for m in range(parity, len(values), 2):
            factor = function(2.0 * math.pi * (m * v % count) / count)
            if abs(factor) > 1e-9:
                term = values[m] if abs(factor - 1.0) < 1e-9 else factor * values[m]
                total = term if total is None else total + term
        return total

    def add(x, y):
        return y if x is None else x if y is None else x + y

    def subtract(x, y):
        return x if y is None else -y if x is None else x - y

    half = count // 2
    out = [None] * count
    for v in range(half // 2 + 1):
        sums = [
            [weighted(function, v, values, parity) for parity in range(2)]
            for function, values in (
                (math.cos, real),
                (math.sin, imag),
                (math.cos, imag),
                (math.sin, real),
            )
        ]
        (p0, p1), (q0, q1), (r0, r1), (u0, u1) = sums
        found = [(v, add(p0, p1), add(q0, q1), add(r0, r1), add(u0, u1))]
        if v < half - v:
            found.append(
                (half - v, subtract(p0, p1), subtract(q1, q0), subtract(r0, r1), subtract(u1, u0))
            )
        for w, p, q, r, u in found:
            out[w] = (subtract(p, q), add(r, u))
            if 0 < w < half:
                out[count - w] = (add(p, q), subtract(r, u))
    return out


def transform(
    arrived, order, order_copy, twist, table, lhs, mixed, terms, field, pad, levels
):
    sources = arrived.shape[0]
    rows, chunks = field.shape[:2]
    pieces = rows // SUB
    group = LANES // pad
    lane = lax.broadcasted_iota(jnp.int32, (SUB * SUB, LANES), 1)
    height = levels * SUB
    for g in range(-(-sources // group)):
        members = [arrived[q].astype(F32) for q in range(g * group, min(sources, (g + 1) * group))]
        for piece in range(pieces):
            value = None
            for i, member in enumerate(members):
                shift = pad * (i - piece) % LANES
                turned = pltpu.roll(member, shift, 1) if shift else member
                value = turned if value is None else jnp.where(lane >= i * pad, turned, value)
            value = value.astype(BF16)
            for c in range(2):
                first = (c * pieces + piece) * height
                lhs[first : first + height, g * LANES : (g + 1) * LANES] = value[
                    c * height : (c + 1) * height
                ]
    half = pieces * height
    near = table.shape[1]
    depth = mixed.shape[0]
    order_copy.wait()
    for m in range(depth):
        mixed[m] = jnp.dot(
            lhs[...], order[:, m * near : (m + 1) * near], preferred_element_type=F32
        )

    def vary(i, carry):
        span = pl.ds(pl.multiple_of(i * 2 * SUB, 2 * SUB), 2 * SUB)
        other = pl.ds(pl.multiple_of(half + i * 2 * SUB, 2 * SUB), 2 * SUB)
        for lo in range(0, near, LANES):
            lanes = slice(lo, lo + LANES)
            real = [mixed[m, span, lanes] for m in range(depth)]
            imag = [mixed[m, other, lanes] for m in range(depth)]
            for v, (x, y) in enumerate(spread(real, imag, chunks)):
                if v:
                    cos, sin = twist[2 * v : 2 * v + 1, lanes], twist[2 * v + 1 : 2 * v + 2, lanes]
                    x, y = x * cos - y * sin, x * sin + y * cos
                for c, value in enumerate((x, y)):
                    high = value.astype(BF16)
                    low = (value - high.astype(F32)).astype(BF16)
                    terms[v, span, c * near + lo : c * near + lo + LANES] = high
                    terms[v, span, (2 + c) * near + lo : (2 + c) * near + lo + LANES] = low
        return carry

    lax.fori_loop(0, half // (2 * SUB), vary, 0)
    parts = SUB // levels

    group = chunks // 2

    def finish(i, carry):
        both = terms[pl.ds(i * group, group)].reshape(group * half, 4 * near)
        high, low = both[:, : 2 * near], both[:, 2 * near :]
        value = jnp.dot(high, table[: 2 * near], preferred_element_type=F32)
        value += jnp.dot(low, table[: 2 * near], preferred_element_type=F32)
        value += jnp.dot(high, table[2 * near :], preferred_element_type=F32)
        for v in range(group):
            for piece in range(pieces):
                tiles = []
                for part in range(parts):
                    for level in range(levels):
                        first = v * half + (piece * levels + level) * SUB
                        lanes = slice(part * LANES, (part + 1) * LANES)
                        tiles.append(value[first : first + SUB, lanes])
                turned = jnp.swapaxes(jnp.stack(tiles, 0), 0, 1)
                for t in range(SUB):
                    field[piece * SUB + t, i * group + v] = turned[t]
        return carry

    lax.fori_loop(0, chunks // group, finish, 0)


def upwind_rows(t, count, old, new, cx, cy, levels):
    chunks = old.shape[1]
    west = [west_of_first(old[t + r, chunks - 1], levels) for r in range(count)]
    first, base = None, None
    for v in range(chunks + 1):
        if v < chunks:
            q = [old[t - 1 + r, v] for r in range(count + 2)]
            flux_lat, flux_lon = [], []
            for r in range(count + 1):
                speed = cy[t + r, v]
                flux_lat.append(jnp.maximum(speed, 0.0) * q[r] + jnp.minimum(speed, 0.0) * q[r + 1])
            for r in range(count):
                speed = cx[t + r, v]
                flux_lon.append(
                    jnp.maximum(speed, 0.0) * west[r] + jnp.minimum(speed, 0.0) * q[r + 1]
                )
            west = q[1 : count + 1]
            first = flux_lon if v == 0 else first
        else:
            flux_lon = [east_of_last(x, levels) for x in first]
        for r in range(count):
            if v > 0:
                new[t + r, v - 1] = base[r] - flux_lon[r]
        if v < chunks:
            base = [q[r + 1] + flux_lon[r] - (flux_lat[r + 1] - flux_lat[r]) for r in range(count)]


def corrective_rows(t, count, old, new, ax, bx, ay, by, levels):
    chunks = old.shape[1]
    span = range(count + 2)

    def inverse(x):
        return pl.reciprocal(jnp.maximum(x, 1.0), approx=True)

    def flux(a, b, gradient, cross, total, step):
        speed = a * gradient - b * cross
        return speed * total - jnp.abs(speed) * step

    here = [old[t - 1 + r, 0] for r in span]
    start = here
    west = [west_of_first(old[t - 1 + r, chunks - 1], levels) for r in span]
    size, size_west = [jnp.abs(x) for x in here], [jnp.abs(x) for x in west]
    first, base = None, None
    for v in range(chunks + 1):
        if v < chunks:
            if v + 1 < chunks:
                east = [old[t - 1 + r, v + 1] for r in span]
            else:
                east = [east_of_last(x, levels) for x in start]
            size_east = [jnp.abs(x) for x in east]
            flux_lat, flux_lon = [], []
            apart = [east[r] - west[r] for r in span]
            sizes_apart = [size_east[r] + size_west[r] for r in span]
            for r in range(count + 1):
                step = here[r + 1] - here[r]
                gradient = step * inverse(size[r + 1] + size[r])
                cross = (apart[r + 1] + apart[r]) * inverse(sizes_apart[r + 1] + sizes_apart[r])
                flux_lat.append(
                    flux(ay[t + r, v], by[t + r, v], gradient, cross, here[r + 1] + here[r], step)
                )
            total = [here[r] + west[r] for r in span]
            sizes = [size[r] + size_west[r] for r in span]
            for r in range(1, count + 1):
                step = here[r] - west[r]
                gradient = step * inverse(sizes[r])
                cross = (total[r + 1] - total[r - 1]) * inverse(sizes[r + 1] + sizes[r - 1])
                flux_lon.append(
                    flux(ax[t + r - 1, v], bx[t + r - 1, v], gradient, cross, total[r], step)
                )
            first = flux_lon if v == 0 else first
        else:
            flux_lon = [east_of_last(x, levels) for x in first]
        for r in range(count):
            if v > 0:
                new[t + r, v - 1] = base[r] - flux_lon[r]
        if v < chunks:
            base = [
                here[r + 1] + flux_lon[r] - (flux_lat[r + 1] - flux_lat[r]) for r in range(count)
            ]
            west, here, size_west, size = here, east, size, size_east


def advect_kernel(pad, arrived, far_order, twist, table, *refs):
    far_fields = refs[:3]
    out, fields, order, lhs, mixed, terms, field, upwind, turned, sems = refs[3:]
    cx, cy, ax, bx, ay, by = [fields.at[i] for i in range(6)]
    levels, band, nlon = out.shape
    rows, chunks = field.shape[:2]
    copies = [pltpu.make_async_copy(far_order, order, sems.at[0])]
    start = 0
    for i, far in enumerate(far_fields):
        place = fields.at[:, pl.ds(start, far.shape[1])]
        copies.append(pltpu.make_async_copy(far, place, sems.at[1 + i]))
        start += far.shape[1]
    for copy in copies:
        copy.start()
    transform(
        arrived, order, copies[0], twist, table, lhs, mixed, terms, field, pad, levels
    )
    for copy in copies[1:]:
        copy.wait()
    outermost = lax.axis_index("wave") == 0

    def clear(where):
        @pl.when(outermost)
        def _():
            where[HALO - 1] = jnp.zeros((chunks, SUB, LANES), F32)

    def one_pass(number, carry):
        start = 2 * number + 1

        def first(i, carry):
            upwind_rows(start + 2 * i, 2, field, upwind, cx, cy, levels)
            return carry

        lax.fori_loop(0, rows // 2 - 1 - 2 * number, first, 0)
        clear(upwind)

        def second(i, carry):
            corrective_rows(start + 1 + 4 * i, 4, upwind, field, ax, bx, ay, by, levels)
            return carry

        lax.fori_loop(0, rows // 4 - 1 - number, second, 0)
        clear(field)
        return carry

    lax.fori_loop(0, PASSES, one_pass, 0)
    span = nlon * levels // SUB
    for block in range(band // SUB):
        first = HALO + block * SUB

        def stand(v, carry, first=first):
            value = jnp.swapaxes(field[pl.ds(first, SUB), v], 0, 1).reshape(SUB * SUB, LANES)
            value = jnp.transpose(jnp.concatenate([value, value], 0))
            turned[pl.ds(v, LANES, stride=chunks), :] = value
            return carry

        lax.fori_loop(0, chunks, stand, 0, unroll=2)
        for n in range(span // LANES):
            value = jnp.transpose(turned[n * LANES : (n + 1) * LANES, :])
            for i in range(SUB):
                lanes = i // levels * span + n * LANES
                out[i % levels, block * SUB : (block + 1) * SUB, lanes : lanes + LANES] = value[
                    i * SUB : (i + 1) * SUB
                ]


def advect(arrived, order, twist, table, fields, shape, pad):
    levels, band, nlon = shape
    rows, chunks = sum(x.shape[1] for x in fields), fields[0].shape[2]
    half = rows * levels
    near = table.shape[1]
    order, *fields = [
        pltpu.with_memory_space_constraint(x, pltpu.HBM) for x in (order, *fields)
    ]
    vmem, far = pl.BlockSpec(memory_space=pltpu.VMEM), pl.BlockSpec(memory_space=pltpu.HBM)
    return pl.pallas_call(
        functools.partial(advect_kernel, pad),
        out_shape=jax.ShapeDtypeStruct(shape, F32),
        in_specs=[vmem, far, vmem, vmem] + [far] * 3,
        scratch_shapes=[
            pltpu.VMEM((6, rows, chunks, SUB, LANES), F32),
            pltpu.VMEM(order.shape, BF16),
            pltpu.VMEM((2 * half, order.shape[0]), BF16),
            pltpu.VMEM((order.shape[1] // near, 2 * half, near), F32),
            pltpu.VMEM((chunks, half, 4 * near), BF16),
            pltpu.VMEM((rows, chunks, SUB, LANES), F32),
            pltpu.VMEM((rows, chunks, SUB, LANES), F32),
            pltpu.VMEM((nlon * levels // SUB, LANES), F32),
            pltpu.SemaphoreType.DMA((4,)),
        ],
        compiler_params=params(40),
        name="advect",
    )(arrived, order, twist, table, *fields)


def fourier_tables(nlon, near):
    chunks = nlon // near
    f = np.arange(near)
    angle = 2.0 * np.pi / nlon * (np.arange(chunks)[:, None] * f[None, :] % nlon)
    twist = np.stack([np.cos(angle), np.sin(angle)], 1).reshape(2 * chunks, near)
    angle = 2.0 * np.pi / near * (f[:, None] * f[None, :] % near)
    whole = np.concatenate([np.cos(angle), -np.sin(angle)], 0).astype(np.float32)
    high = whole.astype(ml_dtypes.bfloat16)
    low = (whole - high.astype(np.float32)).astype(ml_dtypes.bfloat16)
    return twist.astype(np.float32), np.concatenate([high, low], 0)


def order_matrix(wave_table, sources, pad):
    waves = 2 * wave_table.shape[0]
    group = LANES // pad
    numbers = jnp.stack([wave_table, waves - 1 - wave_table], 1).reshape(sources, -1)
    extra = -sources % group
    column = jnp.pad(numbers, ((0, extra), (0, pad - numbers.shape[1])), constant_values=-1)
    column = column.reshape(-1, group * pad)
    column = jnp.pad(column, ((0, 0), (0, LANES - group * pad)), constant_values=-1).reshape(-1, 1)
    weight = jnp.where(column == 0, 1.0, 2.0).astype(BF16)
    return jnp.where(jnp.arange(waves)[None, :] == column, weight, jnp.zeros((), BF16))


def body(spectral, legendre, wave_table, courant_lon, courant_lat):
    wave_count, level_count = lax.axis_size("wave"), lax.axis_size("lev")
    wave_rank, level_rank = lax.axis_index("wave"), lax.axis_index("lev")
    levels, band, nlon = courant_lon.shape
    own = legendre.shape[0]
    waves = 2 * wave_table.shape[0]
    pad = -(-2 * own // SUB) * SUB

    up = [(i, i + 1) for i in range(wave_count - 1)]
    down = [(i + 1, i) for i in range(wave_count - 1)]
    spectral = spectral.reshape((-1,) + spectral.shape[2:])
    half = level_count // 2
    far_blocks = pack(spectral, range(half, level_count), level_count)
    far_blocks, spectral = lax.optimization_barrier((far_blocks, spectral))
    blocks = list(pack(spectral, range(half), level_count)) + list(far_blocks)
    for step in range(1, level_count):
        pairs = [(i, i ^ step) for i in range(level_count)]
        blocks[step] = lax.ppermute(blocks[step], "lev", pairs)
    blocks[1], winds = lax.optimization_barrier((blocks[1], (courant_lon, courant_lat)))
    lower, upper = halos(*winds)
    own_winds = own_courant(*winds)
    below = lax.ppermute(upper, "wave", up)
    above = lax.ppermute(lower, "wave", down)

    own_pairs = lax.dynamic_slice_in_dim(
        wave_table, (wave_rank * level_count + level_rank) * own, own
    )
    turned = jnp.swapaxes(legendre, 1, 2)
    given = (turned, own_pairs, wave_count, waves, pad)
    sums = list(legendre_sums(range(half), blocks[:half], *given))
    order = order_matrix(wave_table, wave_count * level_count, pad)
    sums, order, own_winds = lax.optimization_barrier((sums, order, own_winds))
    for step in range(half, level_count - 1):
        sums += legendre_sums([step], blocks[step : step + 1], *given)
    stacked = legendre_sums([level_count - 1], blocks[-1:], *given, done=tuple(sums))
    arrived = lax.all_to_all(
        stacked.reshape(-1, SUB * SUB, LANES), ("wave", "lev"), 0, 0, tiled=True
    )

    fields = [
        factor_rows(own_winds, received, side, levels)
        for side, received in ((-1, below), (0, None), (1, above))
    ]
    twist, table = fourier_tables(nlon, SUB // levels * LANES)
    return advect(
        arrived, order, jnp.asarray(twist), jnp.asarray(table), fields, courant_lon.shape, pad
    )


def solution(mesh):
    placed = (
        P(None, "lev", "wave", None),
        P(("wave", "lev"), None, None),
        P(),
        P("lev", "wave", None),
        P("lev", "wave", None),
    )
    return jax.shard_map(
        body, mesh=mesh, in_specs=placed, out_specs=P("lev", "wave", None), check_vma=False
    )
```

```python
import functools
import math

import jax
import jax.numpy as jnp
import ml_dtypes
import numpy as np
from jax import lax
from jax.experimental import pallas as pl
from jax.experimental.pallas import tpu as pltpu
from jax.sharding import PartitionSpec as P

PASSES = 4
HALO = 2 * PASSES
SUB = 8
LANES = 128
F32 = jnp.float32
BF16 = jnp.bfloat16


def params(mib):
    return pltpu.CompilerParams(vmem_limit_bytes=mib << 20)


def lane_index():
    return lax.broadcasted_iota(jnp.int32, (SUB, LANES), 1)


def pack_kernel(count, steps, x_ref, *refs):
    turned = refs[-1]
    degrees = x_ref.shape[2]
    own = turned.shape[0] // (count // 2)
    pairs = -(-own // 2)
    whole = degrees // LANES
    me = lax.axis_index("lev")
    there = (me ^ steps[0]) // (count // 2)
    for part in range(2):
        start = part * turned.shape[0]
        first = start // SUB * SUB

        @pl.when(there == part)
        def _(start=start, first=first):
            for group in range(first, start + turned.shape[0], SUB):
                for lo in range(0, degrees, LANES):
                    hi = min(lo + LANES, degrees)
                    tile = [x_ref[i, group : group + SUB, lo:hi].astype(F32) for i in range(SUB)]
                    tile = jnp.swapaxes(jnp.stack(tile, 0), 0, 1)
                    skip = max(start - group, 0)
                    keep = min(start + turned.shape[0] - group, SUB)
                    at = group + skip - start
                    turned[at : at + keep - skip, :, lo:hi] = tile[skip:keep]

    lane = lax.broadcasted_iota(jnp.int32, (2 * SUB, LANES), 1)
    for step, out in zip(steps, refs):
        start = (me ^ step) % (count // 2) * own

        def two(i, start=start):
            return start + 2 * i, start + jnp.minimum(2 * i + 1, own - 1)

        def pair(i, carry, out=out, two=two):
            for n in range(whole):
                both = [turned[slot, :, n * LANES : (n + 1) * LANES] for slot in two(i)]
                row = pl.multiple_of((i * whole + n) * 2 * SUB, 2 * SUB)
                out[pl.ds(row, 2 * SUB), :] = jnp.concatenate(both, 0).astype(BF16)
            return carry

        lax.fori_loop(0, pairs, pair, 0)
        rest = jnp.zeros((2 * SUB, LANES), F32)
        for i in range(pairs):
            last = [turned[slot, :, whole * LANES :] for slot in two(i)]
            rest = jnp.where(lane == i, jnp.concatenate(last, 0), rest)
        out[pairs * whole * 2 * SUB :, :] = rest.astype(BF16)


def pack(spectral, steps, count):
    levels, slots, degrees = spectral.shape
    pairs = -(-slots // count // 2)
    out = jax.ShapeDtypeStruct(((pairs * (degrees // LANES) + 1) * 2 * SUB, LANES), BF16)
    spectral = jnp.pad(spectral, ((0, 0), (0, -slots % (2 * SUB)), (0, 0)))
    return pl.pallas_call(
        functools.partial(pack_kernel, count, steps),
        out_shape=[out] * len(steps),
        scratch_shapes=[pltpu.VMEM((slots // 2, SUB, degrees), F32)],
        compiler_params=params(40),
        name="pack",
    )(spectral)


def legendre_kernel(steps, bands, waves, pad, early, pairs_ref, *refs):
    count = len(steps)
    blocks, table, done = refs[:count], refs[count], refs[count + 1 : count + 1 + early]
    outs, sums = refs[count + 1 + early : -1], refs[-1]
    if early:
        me = lax.axis_index("lev")
        outs = [outs[0].at[:, me ^ step] for step in range(early + count)]
        for value, out in zip(done, outs):
            out[...] = value[...]
        outs = outs[early:]
    own, lats, degrees = table.shape
    whole = degrees // LANES
    wide = sums.shape[-1]
    band = lats // bands
    pieces = band // SUB + 2
    if wide > lats:
        sums[...] = jnp.zeros_like(sums)
    elif 2 * own < pad:
        sums[:, 2 * own :] = jnp.zeros((count, pad - 2 * own, SUB, wide), F32)

    def pair(i, carry):
        rows = []
        for block in blocks:
            parts = []
            for n in range(whole):
                first = pl.multiple_of((i * whole + n) * 2 * SUB, 2 * SUB)
                parts.append(block[pl.ds(first, 2 * SUB), :].astype(F32))
            rest = block[block.shape[0] - 2 * SUB :, :].astype(F32)
            parts.append(pltpu.roll(rest, (LANES - i) % LANES, 1)[:, : degrees - whole * LANES])
            rows.append(jnp.concatenate(parts, 1))
        rows = jnp.concatenate(rows, 0)
        row = lax.broadcasted_iota(jnp.int32, rows.shape, 0) % (2 * SUB)
        degree = lax.broadcasted_iota(jnp.int32, rows.shape, 1)
        second = jnp.minimum(2 * i + 1, own - 1)
        bound = waves - jnp.where(row < SUB, pairs_ref[2 * i], pairs_ref[second])
        low = jnp.where(degree < bound, rows, 0.0)
        both = jnp.concatenate([low, rows - low], 0).astype(BF16)
        for j in range(2):
            got = lax.dot_general(
                both,
                table[second if j else 2 * i],
                (((1,), (1,)), ((), ())),
                preferred_element_type=F32,
            )
            for half in range(2):
                for d in range(count):
                    first = (half * count + d) * 2 * SUB + j * SUB
                    sums[d, 4 * i + 2 * j + half, :, :lats] = got[first : first + SUB]
        return carry

    lax.fori_loop(0, -(-own // 2), pair, 0, unroll=5)
    lane = lane_index()
    nothing = jnp.zeros((SUB, LANES), F32)
    for d in range(count):
        tiles = [
            [jnp.swapaxes(sums[d, 8 * g : 8 * g + 8, :, k : k + LANES], 0, 1) for k in range(0, wide, LANES)]
            for g in range(pad // SUB)
        ]
        stood = []
        for i in range(SUB):
            once = [jnp.concatenate([tile[i] for tile in row], 1) for row in tiles]
            spare = (LANES - pieces * pad) // SUB
            tall = once * pieces + [jnp.zeros((SUB, wide), F32)] * spare
            stood.append(jnp.transpose(jnp.concatenate(tall, 0)))
        for w in range(bands):
            for i in range(0, SUB, 2):
                two = []
                for value in stood[i : i + 2]:
                    tile = nothing
                    for piece in reversed(range(pieces)):
                        first = w * band + (piece - 1) * SUB
                        there = value[first : first + SUB] if 0 <= first < lats else nothing
                        tile = there if piece == pieces - 1 else jnp.where(
                            lane < (piece + 1) * pad, there, tile
                        )
                    two.append(tile)
                outs[d][w, i * SUB : (i + 2) * SUB, :] = jnp.concatenate(two, 0).astype(BF16)


def legendre_sums(steps, blocks, table, own_pairs, bands, waves, pad, done=()):
    own, lats, degrees = table.shape
    wide = -(-lats // LANES) * LANES
    outs = [jax.ShapeDtypeStruct((bands, SUB * SUB, LANES), BF16)] * len(steps)
    if done:
        outs = jax.ShapeDtypeStruct((bands, len(done) + len(steps), SUB * SUB, LANES), BF16)
    vmem = pl.BlockSpec(memory_space=pltpu.VMEM)
    return pl.pallas_call(
        functools.partial(legendre_kernel, steps, bands, waves, pad, len(done)),
        out_shape=outs,
        in_specs=[pl.BlockSpec(memory_space=pltpu.SMEM)] + [vmem] * (len(steps) + 1 + len(done)),
        scratch_shapes=[pltpu.VMEM((len(steps), pad, SUB, wide), F32)],
        compiler_params=params(40),
        name="legendre",
    )(own_pairs, *blocks, table, *done)


def west_of_first(last_chunk, levels):
    turned = pltpu.roll(last_chunk, 1, 1)
    return jnp.where(lane_index() == 0, pltpu.roll(turned, levels, 0), turned)


def east_of_last(first_chunk, levels):
    turned = pltpu.roll(first_chunk, LANES - 1, 1)
    return jnp.where(lane_index() == LANES - 1, pltpu.roll(turned, SUB - levels, 0), turned)


def halo_kernel(lon, lat, *refs):
    levels, band = lon.shape[:2]
    for halo, start in zip(refs, (0, band - HALO)):
        for field, wind in enumerate((lon, lat)):
            for level in range(0, levels, 2):
                both = [wind[level + k, start : start + HALO, :] for k in range(2)]
                row = (field * levels + level) * HALO
                halo[row : row + 2 * HALO, :] = jnp.concatenate(both, 0).astype(BF16)


def halos(lon, lat):
    levels, band, nlon = lon.shape
    halo = jax.ShapeDtypeStruct((2 * levels * HALO, nlon), BF16)
    made = pl.pallas_call(
        halo_kernel,
        out_shape=[halo] * (1 if band == HALO else 2),
        compiler_params=params(12),
        name="halos",
    )(lon, lat)
    return made[0], made[-1]


def turn(tiles_of, rows, start, turned):
    chunks = rows.shape[2]

    def stand(n, carry):
        first = pl.multiple_of(n * LANES, LANES)
        turned[pl.ds(first, LANES), :] = jnp.transpose(jnp.concatenate(tiles_of(n), 0))
        return carry

    def lie(v, carry):
        value = jnp.transpose(turned[pl.ds(v, LANES, stride=chunks), :])
        for field in range(2):
            both = value[field * SUB * SUB : (field + 1) * SUB * SUB]
            both = jnp.swapaxes(both.reshape(SUB, SUB, LANES), 0, 1)
            for t in range(SUB):
                rows[field, start + t, v] = both[t]
        return carry

    lax.fori_loop(0, turned.shape[0] // LANES, stand, 0, unroll=4)
    lax.fori_loop(0, chunks, lie, 0, unroll=4)


def lanes_of(part, n, span):
    return pl.ds(pl.multiple_of(part * span + n * LANES, LANES), LANES)


def own_courant_kernel(lon, lat, own, rows, turned, sem):
    levels, band, _ = lon.shape
    for start in range(0, band, SUB):

        def tiles_of(n, start=start):
            return [
                wind[level, start : start + SUB, lanes_of(part, n, turned.shape[0])]
                for wind in (lon, lat)
                for part in range(SUB // levels)
                for level in range(levels)
            ]

        turn(tiles_of, rows, start, turned)
    copy = pltpu.make_async_copy(rows, own, sem)
    copy.start()
    copy.wait()


def own_courant(lon, lat):
    levels, band, nlon = lon.shape
    parts = SUB // levels
    shape = (2, band, nlon // (parts * LANES), SUB, LANES)
    return pl.pallas_call(
        own_courant_kernel,
        out_shape=pltpu.HBM(shape, F32),
        out_specs=pl.BlockSpec(memory_space=pltpu.HBM),
        scratch_shapes=[
            pltpu.VMEM(shape, F32),
            pltpu.VMEM((nlon // parts, LANES), F32),
            pltpu.SemaphoreType.DMA,
        ],
        compiler_params=params(16),
        name="own_courant",
    )(lon, lat)


def factor_kernel(levels, side, own, *refs):
    far_out, fields, sems = refs[1:4] if side else refs
    cx, cy, ax, bx, ay, by = [fields.at[i] for i in range(6)]
    rows, chunks = fields.shape[1:3]
    band = own.shape[1]
    if side:
        start, at = (0, HALO) if side < 0 else (band - 2, 0)
        source, target = own.at[:, pl.ds(start, 2)], fields.at[pl.ds(0, 2), pl.ds(at, 2)]
    else:
        source, target = own, fields.at[pl.ds(0, 2)]
    copy = pltpu.make_async_copy(source, target, sems.at[0])
    copy.start()
    if side:
        received, turned = refs[0], refs[-1]

        def tiles_of(n):
            height = levels * SUB
            return [
                received[wind * height : (wind + 1) * height, lanes_of(part, n, turned.shape[0])].astype(F32)
                for wind in range(2)
                for part in range(SUB // levels)
            ]

        turn(tiles_of, fields, 0 if side < 0 else 2, turned)
    copy.wait()
    low = 0 if side < 0 else 1
    height = far_out.shape[1]
    copies = [
        pltpu.make_async_copy(
            fields.at[pl.ds(i, count), pl.ds(low, height)],
            far_out.at[pl.ds(i, count)],
            sems.at[1 + k],
        )
        for k, (i, count) in enumerate(((0, 2), (2, 4)))
    ]
    copies[0].start()
    if side:
        for i in range(2, 6):
            fields[i, 0 if side < 0 else rows - 1] = jnp.zeros((chunks, SUB, LANES), F32)

    def factors(t, carry):
        u = [cx[t, v] for v in range(chunks)]
        w = [cy[t, v] for v in range(chunks)]
        near = [w[v] + cy[t + 1, v] for v in range(chunks)]
        west = [west_of_first(near[-1], levels)] + near[:-1]
        for v in range(chunks):
            ax[t, v] = jnp.abs(u[v]) - u[v] * u[v]
            bx[t, v] = 0.125 * u[v] * (near[v] + west[v])
        near = [u[v] + cx[t - 1, v] for v in range(chunks)]
        east = near[1:] + [east_of_last(near[0], levels)]
        for v in range(chunks):
            ay[t, v] = jnp.abs(w[v]) - w[v] * w[v]
            by[t, v] = 0.125 * w[v] * (near[v] + east[v])
        return carry

    lax.fori_loop(1, rows - 1, factors, 0)
    copies[1].start()
    for copy in copies:
        copy.wait()


def factor_rows(own, received, side, levels):
    _, band, chunks, _, _ = own.shape
    rows = HALO + 2 if side else band
    out = HALO + 1 if side else band - 2
    vmem, far = pl.BlockSpec(memory_space=pltpu.VMEM), pl.BlockSpec(memory_space=pltpu.HBM)
    extra = (received,) if side else ()
    return pl.pallas_call(
        functools.partial(factor_kernel, levels, side),
        out_shape=pltpu.HBM((6, out, chunks, SUB, LANES), F32),
        in_specs=[far] + [vmem] * len(extra),
        out_specs=far,
        scratch_shapes=[
            pltpu.VMEM((6, rows, chunks, SUB, LANES), F32),
            pltpu.SemaphoreType.DMA((3,)),
        ]
        + [pltpu.VMEM((chunks * LANES, LANES), F32)] * len(extra),
        compiler_params=params(16),
        cost_estimate=pl.CostEstimate(
            flops=30_000_000_000 if side > 0 else 1_000_000_000,
            bytes_accessed=8_000_000,
            transcendentals=0,
        ),
        name="factors",
    )(pltpu.with_memory_space_constraint(own, pltpu.HBM), *extra)


def spread(real, imag, count):
    def weighted(function, v, values, parity):
        total = None
        for m in range(parity, len(values), 2):
            factor = function(2.0 * math.pi * (m * v % count) / count)
            if abs(factor) > 1e-9:
                term = values[m] if abs(factor - 1.0) < 1e-9 else factor * values[m]
                total = term if total is None else total + term
        return total

    def add(x, y):
        return y if x is None else x if y is None else x + y

    def subtract(x, y):
        return x if y is None else -y if x is None else x - y

    half = count // 2
    out = [None] * count
    for v in range(half // 2 + 1):
        sums = [
            [weighted(function, v, values, parity) for parity in range(2)]
            for function, values in (
                (math.cos, real),
                (math.sin, imag),
                (math.cos, imag),
                (math.sin, real),
            )
        ]
        (p0, p1), (q0, q1), (r0, r1), (u0, u1) = sums
        found = [(v, add(p0, p1), add(q0, q1), add(r0, r1), add(u0, u1))]
        if v < half - v:
            found.append(
                (half - v, subtract(p0, p1), subtract(q1, q0), subtract(r0, r1), subtract(u1, u0))
            )
        for w, p, q, r, u in found:
            out[w] = (subtract(p, q), add(r, u))
            if 0 < w < half:
                out[count - w] = (add(p, q), subtract(r, u))
    return out


def transform(
    arrived, order, order_copy, twist, table, lhs, mixed, terms, field, pad, levels
):
    sources = arrived.shape[0]
    rows, chunks = field.shape[:2]
    pieces = rows // SUB
    group = LANES // pad
    lane = lax.broadcasted_iota(jnp.int32, (SUB * SUB, LANES), 1)
    height = levels * SUB
    for g in range(-(-sources // group)):
        members = [arrived[q].astype(F32) for q in range(g * group, min(sources, (g + 1) * group))]
        for piece in range(pieces):
            value = None
            for i, member in enumerate(members):
                shift = pad * (i - piece) % LANES
                turned = pltpu.roll(member, shift, 1) if shift else member
                value = turned if value is None else jnp.where(lane >= i * pad, turned, value)
            value = value.astype(BF16)
            for c in range(2):
                first = (c * pieces + piece) * height
                lhs[first : first + height, g * LANES : (g + 1) * LANES] = value[
                    c * height : (c + 1) * height
                ]
    half = pieces * height
    near = table.shape[1]
    depth = mixed.shape[0]
    order_copy.wait()
    for m in range(depth):
        mixed[m] = jnp.dot(
            lhs[...], order[:, m * near : (m + 1) * near], preferred_element_type=F32
        )

    def vary(i, carry):
        span = pl.ds(pl.multiple_of(i * 2 * SUB, 2 * SUB), 2 * SUB)
        other = pl.ds(pl.multiple_of(half + i * 2 * SUB, 2 * SUB), 2 * SUB)
        for lo in range(0, near, LANES):
            lanes = slice(lo, lo + LANES)
            real = [mixed[m, span, lanes] for m in range(depth)]
            imag = [mixed[m, other, lanes] for m in range(depth)]
            for v, (x, y) in enumerate(spread(real, imag, chunks)):
                if v:
                    cos, sin = twist[2 * v : 2 * v + 1, lanes], twist[2 * v + 1 : 2 * v + 2, lanes]
                    x, y = x * cos - y * sin, x * sin + y * cos
                for c, value in enumerate((x, y)):
                    high = value.astype(BF16)
                    low = (value - high.astype(F32)).astype(BF16)
                    terms[v, span, c * near + lo : c * near + lo + LANES] = high
                    terms[v, span, (2 + c) * near + lo : (2 + c) * near + lo + LANES] = low
        return carry

    lax.fori_loop(0, half // (2 * SUB), vary, 0)
    parts = SUB // levels

    group = chunks // 2

    def finish(i, carry):
        both = terms[pl.ds(i * group, group)].reshape(group * half, 4 * near)
        high, low = both[:, : 2 * near], both[:, 2 * near :]
        value = jnp.dot(high, table[: 2 * near], preferred_element_type=F32)
        value += jnp.dot(low, table[: 2 * near], preferred_element_type=F32)
        value += jnp.dot(high, table[2 * near :], preferred_element_type=F32)
        for v in range(group):
            for piece in range(pieces):
                tiles = []
                for part in range(parts):
                    for level in range(levels):
                        first = v * half + (piece * levels + level) * SUB
                        lanes = slice(part * LANES, (part + 1) * LANES)
                        tiles.append(value[first : first + SUB, lanes])
                turned = jnp.swapaxes(jnp.stack(tiles, 0), 0, 1)
                for t in range(SUB):
                    field[piece * SUB + t, i * group + v] = turned[t]
        return carry

    lax.fori_loop(0, chunks // group, finish, 0)


def donor(a, b, speed):
    return speed * jnp.where(speed > 0.0, a, b)


def upwind_rows(t, count, old, new, cx, cy, levels):
    chunks = old.shape[1]
    west = [west_of_first(old[t + r, chunks - 1], levels) for r in range(count)]
    first, base = None, None
    for v in range(chunks + 1):
        if v < chunks:
            q = [old[t - 1 + r, v] for r in range(count + 2)]
            flux_lat, flux_lon = [], []
            for r in range(count + 1):
                speed = cy[t + r, v]
                flux_lat.append(donor(q[r], q[r + 1], speed))
            for r in range(count):
                speed = cx[t + r, v]
                flux_lon.append(donor(west[r], q[r + 1], speed))
            west = q[1 : count + 1]
            first = flux_lon if v == 0 else first
        else:
            flux_lon = [east_of_last(x, levels) for x in first]
        for r in range(count):
            if v > 0:
                new[t + r, v - 1] = base[r] - flux_lon[r]
        if v < chunks:
            base = [q[r + 1] + flux_lon[r] - (flux_lat[r + 1] - flux_lat[r]) for r in range(count)]


def corrective_rows(t, count, old, new, ax, bx, ay, by, levels):
    chunks = old.shape[1]
    span = range(count + 2)

    def inverse(x):
        return pl.reciprocal(jnp.maximum(x, 1.0), approx=True)

    here = [old[t - 1 + r, 0] for r in span]
    start = here
    west = [west_of_first(old[t - 1 + r, chunks - 1], levels) for r in span]
    size, size_west = [jnp.abs(x) for x in here], [jnp.abs(x) for x in west]
    first, base = None, None
    for v in range(chunks + 1):
        if v < chunks:
            if v + 1 < chunks:
                east = [old[t - 1 + r, v + 1] for r in span]
            else:
                east = [east_of_last(x, levels) for x in start]
            size_east = [jnp.abs(x) for x in east]
            flux_lat, flux_lon = [], []
            apart = [east[r] - west[r] for r in span]
            sizes_apart = [size_east[r] + size_west[r] for r in span]
            for r in range(count + 1):
                step = here[r + 1] - here[r]
                gradient = step * inverse(size[r + 1] + size[r])
                cross = (apart[r + 1] + apart[r]) * inverse(sizes_apart[r + 1] + sizes_apart[r])
                speed = ay[t + r, v] * gradient - by[t + r, v] * cross
                flux_lat.append(donor(here[r], here[r + 1], speed))
            total = [here[r] + west[r] for r in span]
            sizes = [size[r] + size_west[r] for r in span]
            for r in range(1, count + 1):
                step = here[r] - west[r]
                gradient = step * inverse(sizes[r])
                cross = (total[r + 1] - total[r - 1]) * inverse(sizes[r + 1] + sizes[r - 1])
                speed = ax[t + r - 1, v] * gradient - bx[t + r - 1, v] * cross
                flux_lon.append(donor(west[r], here[r], speed))
            first = flux_lon if v == 0 else first
        else:
            flux_lon = [east_of_last(x, levels) for x in first]
        for r in range(count):
            if v > 0:
                new[t + r, v - 1] = base[r] - flux_lon[r]
        if v < chunks:
            base = [
                here[r + 1] + flux_lon[r] - (flux_lat[r + 1] - flux_lat[r]) for r in range(count)
            ]
            west, here, size_west, size = here, east, size, size_east


def advect_kernel(pad, arrived, far_order, twist, table, *refs):
    far_fields = refs[:3]
    out, fields, order, lhs, mixed, terms, field, upwind, turned, sems = refs[3:]
    cx, cy, ax, bx, ay, by = [fields.at[i] for i in range(6)]
    levels, band, nlon = out.shape
    rows, chunks = field.shape[:2]
    copies = [pltpu.make_async_copy(far_order, order, sems.at[0])]
    start = 0
    for i, far in enumerate(far_fields):
        place = fields.at[:, pl.ds(start, far.shape[1])]
        copies.append(pltpu.make_async_copy(far, place, sems.at[1 + i]))
        start += far.shape[1]
    for copy in copies:
        copy.start()
    transform(
        arrived, order, copies[0], twist, table, lhs, mixed, terms, field, pad, levels
    )
    for copy in copies[1:]:
        copy.wait()
    outermost = lax.axis_index("wave") == 0

    def clear(where):
        @pl.when(outermost)
        def _():
            where[HALO - 1] = jnp.zeros((chunks, SUB, LANES), F32)

    def one_pass(number):
        start, height = 2 * number + 1, rows // 2 - 1 - 2 * number

        def first(i, carry):
            upwind_rows(start + height * i, height, field, upwind, cx, cy, levels)
            return carry

        lax.fori_loop(0, 2, first, 0)
        clear(upwind)

        def second(i, carry):
            at = start + 1 + (height - 1) * i
            corrective_rows(at, height - 1, upwind, field, ax, bx, ay, by, levels)
            return carry

        lax.fori_loop(0, 2, second, 0)
        clear(field)

    for number in range(PASSES):
        one_pass(number)
    span = nlon * levels // SUB
    for block in range(band // SUB):
        first = HALO + block * SUB

        def stand(v, carry, first=first):
            value = jnp.swapaxes(field[pl.ds(first, SUB), v], 0, 1).reshape(SUB * SUB, LANES)
            value = jnp.transpose(jnp.concatenate([value, value], 0))
            turned[pl.ds(v, LANES, stride=chunks), :] = value
            return carry

        lax.fori_loop(0, chunks, stand, 0, unroll=2)
        for n in range(span // LANES):
            value = jnp.transpose(turned[n * LANES : (n + 1) * LANES, :])
            for i in range(SUB):
                lanes = i // levels * span + n * LANES
                out[i % levels, block * SUB : (block + 1) * SUB, lanes : lanes + LANES] = value[
                    i * SUB : (i + 1) * SUB
                ]


def advect(arrived, order, twist, table, fields, shape, pad):
    levels, band, nlon = shape
    rows, chunks = sum(x.shape[1] for x in fields), fields[0].shape[2]
    half = rows * levels
    near = table.shape[1]
    order, *fields = [
        pltpu.with_memory_space_constraint(x, pltpu.HBM) for x in (order, *fields)
    ]
    vmem, far = pl.BlockSpec(memory_space=pltpu.VMEM), pl.BlockSpec(memory_space=pltpu.HBM)
    return pl.pallas_call(
        functools.partial(advect_kernel, pad),
        out_shape=jax.ShapeDtypeStruct(shape, F32),
        in_specs=[vmem, far, vmem, vmem] + [far] * 3,
        scratch_shapes=[
            pltpu.VMEM((6, rows, chunks, SUB, LANES), F32),
            pltpu.VMEM(order.shape, BF16),
            pltpu.VMEM((2 * half, order.shape[0]), BF16),
            pltpu.VMEM((order.shape[1] // near, 2 * half, near), F32),
            pltpu.VMEM((chunks, half, 4 * near), BF16),
            pltpu.VMEM((rows, chunks, SUB, LANES), F32),
            pltpu.VMEM((rows, chunks, SUB, LANES), F32),
            pltpu.VMEM((nlon * levels // SUB, LANES), F32),
            pltpu.SemaphoreType.DMA((4,)),
        ],
        compiler_params=params(40),
        name="advect",
    )(arrived, order, twist, table, *fields)


def fourier_tables(nlon, near):
    chunks = nlon // near
    f = np.arange(near)
    angle = 2.0 * np.pi / nlon * (np.arange(chunks)[:, None] * f[None, :] % nlon)
    twist = np.stack([np.cos(angle), np.sin(angle)], 1).reshape(2 * chunks, near)
    angle = 2.0 * np.pi / near * (f[:, None] * f[None, :] % near)
    whole = np.concatenate([np.cos(angle), -np.sin(angle)], 0).astype(np.float32)
    high = whole.astype(ml_dtypes.bfloat16)
    low = (whole - high.astype(np.float32)).astype(ml_dtypes.bfloat16)
    return twist.astype(np.float32), np.concatenate([high, low], 0)


def order_matrix(wave_table, sources, pad):
    waves = 2 * wave_table.shape[0]
    group = LANES // pad
    numbers = jnp.stack([wave_table, waves - 1 - wave_table], 1).reshape(sources, -1)
    extra = -sources % group
    column = jnp.pad(numbers, ((0, extra), (0, pad - numbers.shape[1])), constant_values=-1)
    column = column.reshape(-1, group * pad)
    column = jnp.pad(column, ((0, 0), (0, LANES - group * pad)), constant_values=-1).reshape(-1, 1)
    weight = jnp.where(column == 0, 1.0, 2.0).astype(BF16)
    return jnp.where(jnp.arange(waves)[None, :] == column, weight, jnp.zeros((), BF16))


def body(spectral, legendre, wave_table, courant_lon, courant_lat):
    wave_count, level_count = lax.axis_size("wave"), lax.axis_size("lev")
    wave_rank, level_rank = lax.axis_index("wave"), lax.axis_index("lev")
    levels, band, nlon = courant_lon.shape
    own = legendre.shape[0]
    waves = 2 * wave_table.shape[0]
    pad = -(-2 * own // SUB) * SUB

    up = [(i, i + 1) for i in range(wave_count - 1)]
    down = [(i + 1, i) for i in range(wave_count - 1)]
    spectral = spectral.reshape((-1,) + spectral.shape[2:])
    half = level_count // 2
    far_blocks = pack(spectral, range(half, level_count), level_count)
    far_blocks, spectral = lax.optimization_barrier((far_blocks, spectral))
    blocks = list(pack(spectral, range(half), level_count)) + list(far_blocks)
    for step in range(1, level_count):
        pairs = [(i, i ^ step) for i in range(level_count)]
        blocks[step] = lax.ppermute(blocks[step], "lev", pairs)
    blocks[1], winds = lax.optimization_barrier((blocks[1], (courant_lon, courant_lat)))
    lower, upper = halos(*winds)
    own_winds = own_courant(*winds)
    below = lax.ppermute(upper, "wave", up)
    above = lax.ppermute(lower, "wave", down)

    own_pairs = lax.dynamic_slice_in_dim(
        wave_table, (wave_rank * level_count + level_rank) * own, own
    )
    turned = jnp.swapaxes(legendre, 1, 2)
    given = (turned, own_pairs, wave_count, waves, pad)
    sums = list(legendre_sums(range(level_count - 1), blocks[:-1], *given))
    order = order_matrix(wave_table, wave_count * level_count, pad)
    sums, order, own_winds = lax.optimization_barrier((sums, order, own_winds))
    stacked = legendre_sums([level_count - 1], blocks[-1:], *given, done=tuple(sums))
    arrived = lax.all_to_all(
        stacked.reshape(-1, SUB * SUB, LANES), ("wave", "lev"), 0, 0, tiled=True
    )

    fields = [
        factor_rows(own_winds, received, side, levels)
        for side, received in ((-1, below), (0, None), (1, above))
    ]
    twist, table = fourier_tables(nlon, SUB // levels * LANES)
    return advect(
        arrived, order, jnp.asarray(twist), jnp.asarray(table), fields, courant_lon.shape, pad
    )


def solution(mesh):
    placed = (
        P(None, "lev", "wave", None),
        P(("wave", "lev"), None, None),
        P(),
        P("lev", "wave", None),
        P("lev", "wave", None),
    )
    return jax.shard_map(
        body, mesh=mesh, in_specs=placed, out_specs=P("lev", "wave", None), check_vma=False
    )
```

```python
import functools
import math

import jax
import jax.numpy as jnp
import ml_dtypes
import numpy as np
from jax import lax
from jax.experimental import pallas as pl
from jax.experimental.pallas import tpu as pltpu
from jax.sharding import PartitionSpec as P

PASSES = 4
HALO = 2 * PASSES
SUB = 8
LANES = 128
F32 = jnp.float32
BF16 = jnp.bfloat16


def params(mib):
    return pltpu.CompilerParams(vmem_limit_bytes=mib << 20)


def lane_index():
    return lax.broadcasted_iota(jnp.int32, (SUB, LANES), 1)


def pack_kernel(count, steps, x_ref, *refs):
    turned = refs[-1]
    degrees = x_ref.shape[2]
    own = turned.shape[0] // (count // 2)
    pairs = -(-own // 2)
    whole = degrees // LANES
    me = lax.axis_index("lev")
    there = (me ^ steps[0]) // (count // 2)
    for part in range(2):
        start = part * turned.shape[0]
        first = start // SUB * SUB

        @pl.when(there == part)
        def _(start=start, first=first):
            for group in range(first, start + turned.shape[0], SUB):
                for lo in range(0, degrees, LANES):
                    hi = min(lo + LANES, degrees)
                    tile = [x_ref[i, group : group + SUB, lo:hi].astype(F32) for i in range(SUB)]
                    tile = jnp.swapaxes(jnp.stack(tile, 0), 0, 1)
                    skip = max(start - group, 0)
                    keep = min(start + turned.shape[0] - group, SUB)
                    at = group + skip - start
                    turned[at : at + keep - skip, :, lo:hi] = tile[skip:keep]

    lane = lax.broadcasted_iota(jnp.int32, (2 * SUB, LANES), 1)
    for step, out in zip(steps, refs):
        start = (me ^ step) % (count // 2) * own

        def two(i, start=start):
            return start + 2 * i, start + jnp.minimum(2 * i + 1, own - 1)

        def pair(i, carry, out=out, two=two):
            for n in range(whole):
                both = [turned[slot, :, n * LANES : (n + 1) * LANES] for slot in two(i)]
                row = pl.multiple_of((i * whole + n) * 2 * SUB, 2 * SUB)
                out[pl.ds(row, 2 * SUB), :] = jnp.concatenate(both, 0).astype(BF16)
            return carry

        lax.fori_loop(0, pairs, pair, 0)
        rest = jnp.zeros((2 * SUB, LANES), F32)
        for i in range(pairs):
            last = [turned[slot, :, whole * LANES :] for slot in two(i)]
            rest = jnp.where(lane == i, jnp.concatenate(last, 0), rest)
        out[pairs * whole * 2 * SUB :, :] = rest.astype(BF16)


def pack(spectral, steps, count):
    levels, slots, degrees = spectral.shape
    pairs = -(-slots // count // 2)
    out = jax.ShapeDtypeStruct(((pairs * (degrees // LANES) + 1) * 2 * SUB, LANES), BF16)
    spectral = jnp.pad(spectral, ((0, 0), (0, -slots % (2 * SUB)), (0, 0)))
    return pl.pallas_call(
        functools.partial(pack_kernel, count, steps),
        out_shape=[out] * len(steps),
        scratch_shapes=[pltpu.VMEM((slots // 2, SUB, degrees), F32)],
        compiler_params=params(40),
        name="pack",
    )(spectral)


def legendre_kernel(steps, bands, waves, pad, early, pairs_ref, *refs):
    count = len(steps)
    blocks, table, done = refs[:count], refs[count], refs[count + 1 : count + 1 + early]
    outs, sums = refs[count + 1 + early : -1], refs[-1]
    if early:
        me = lax.axis_index("lev")
        outs = [outs[0].at[:, me ^ step] for step in range(early + count)]
        for value, out in zip(done, outs):
            out[...] = value[...]
        outs = outs[early:]
    own, lats, degrees = table.shape
    whole = degrees // LANES
    wide = sums.shape[-1]
    band = lats // bands
    pieces = band // SUB + 2
    if wide > lats:
        sums[...] = jnp.zeros_like(sums)
    elif 2 * own < pad:
        sums[:, 2 * own :] = jnp.zeros((count, pad - 2 * own, SUB, wide), F32)

    def pair(i, carry):
        rows = []
        for block in blocks:
            parts = []
            for n in range(whole):
                first = pl.multiple_of((i * whole + n) * 2 * SUB, 2 * SUB)
                parts.append(block[pl.ds(first, 2 * SUB), :].astype(F32))
            rest = block[block.shape[0] - 2 * SUB :, :].astype(F32)
            parts.append(pltpu.roll(rest, (LANES - i) % LANES, 1)[:, : degrees - whole * LANES])
            rows.append(jnp.concatenate(parts, 1))
        rows = jnp.concatenate(rows, 0)
        row = lax.broadcasted_iota(jnp.int32, rows.shape, 0) % (2 * SUB)
        degree = lax.broadcasted_iota(jnp.int32, rows.shape, 1)
        second = jnp.minimum(2 * i + 1, own - 1)
        bound = waves - jnp.where(row < SUB, pairs_ref[2 * i], pairs_ref[second])
        low = jnp.where(degree < bound, rows, 0.0)
        both = jnp.concatenate([low, rows - low], 0).astype(BF16)
        for j in range(2):
            got = lax.dot_general(
                both,
                table[second if j else 2 * i],
                (((1,), (1,)), ((), ())),
                preferred_element_type=F32,
            )
            for half in range(2):
                for d in range(count):
                    first = (half * count + d) * 2 * SUB + j * SUB
                    sums[d, 4 * i + 2 * j + half, :, :lats] = got[first : first + SUB]
        return carry

    lax.fori_loop(0, -(-own // 2), pair, 0, unroll=5)
    lane = lane_index()
    nothing = jnp.zeros((SUB, LANES), F32)
    for d in range(count):
        tiles = [
            [jnp.swapaxes(sums[d, 8 * g : 8 * g + 8, :, k : k + LANES], 0, 1) for k in range(0, wide, LANES)]
            for g in range(pad // SUB)
        ]
        stood = []
        for i in range(SUB):
            once = [jnp.concatenate([tile[i] for tile in row], 1) for row in tiles]
            spare = (LANES - pieces * pad) // SUB
            tall = once * pieces + [jnp.zeros((SUB, wide), F32)] * spare
            stood.append(jnp.transpose(jnp.concatenate(tall, 0)))
        for w in range(bands):
            for i in range(0, SUB, 2):
                two = []
                for value in stood[i : i + 2]:
                    tile = nothing
                    for piece in reversed(range(pieces)):
                        first = w * band + (piece - 1) * SUB
                        there = value[first : first + SUB] if 0 <= first < lats else nothing
                        tile = there if piece == pieces - 1 else jnp.where(
                            lane < (piece + 1) * pad, there, tile
                        )
                    two.append(tile)
                outs[d][w, i * SUB : (i + 2) * SUB, :] = jnp.concatenate(two, 0).astype(BF16)


def legendre_sums(steps, blocks, table, own_pairs, bands, waves, pad, done=()):
    own, lats, degrees = table.shape
    wide = -(-lats // LANES) * LANES
    outs = [jax.ShapeDtypeStruct((bands, SUB * SUB, LANES), BF16)] * len(steps)
    if done:
        outs = jax.ShapeDtypeStruct((bands, len(done) + len(steps), SUB * SUB, LANES), BF16)
    vmem = pl.BlockSpec(memory_space=pltpu.VMEM)
    return pl.pallas_call(
        functools.partial(legendre_kernel, steps, bands, waves, pad, len(done)),
        out_shape=outs,
        in_specs=[pl.BlockSpec(memory_space=pltpu.SMEM)] + [vmem] * (len(steps) + 1 + len(done)),
        scratch_shapes=[pltpu.VMEM((len(steps), pad, SUB, wide), F32)],
        compiler_params=params(40),
        name="legendre",
    )(own_pairs, *blocks, table, *done)


def west_of_first(last_chunk, levels):
    turned = pltpu.roll(last_chunk, 1, 1)
    return jnp.where(lane_index() == 0, pltpu.roll(turned, levels, 0), turned)


def east_of_last(first_chunk, levels):
    turned = pltpu.roll(first_chunk, LANES - 1, 1)
    return jnp.where(lane_index() == LANES - 1, pltpu.roll(turned, SUB - levels, 0), turned)


def turn(tiles_of, rows, start, turned):
    chunks = rows.shape[2]

    def stand(n, carry):
        first = pl.multiple_of(n * LANES, LANES)
        turned[pl.ds(first, LANES), :] = jnp.transpose(jnp.concatenate(tiles_of(n), 0))
        return carry

    def lie(v, carry):
        value = jnp.transpose(turned[pl.ds(v, LANES, stride=chunks), :])
        for field in range(2):
            both = value[field * SUB * SUB : (field + 1) * SUB * SUB]
            both = jnp.swapaxes(both.reshape(SUB, SUB, LANES), 0, 1)
            for t in range(SUB):
                rows[field, start + t, v] = both[t]
        return carry

    lax.fori_loop(0, turned.shape[0] // LANES, stand, 0, unroll=4)
    lax.fori_loop(0, chunks, lie, 0, unroll=4)


def lanes_of(part, n, span):
    return pl.ds(pl.multiple_of(part * span + n * LANES, LANES), LANES)


def add_factors(fields, levels, start, stop):
    cx, cy, ax, bx, ay, by = [fields.at[i] for i in range(6)]
    chunks = fields.shape[2]

    def factors(t, carry):
        u = [cx[t, v] for v in range(chunks)]
        w = [cy[t, v] for v in range(chunks)]
        near = [w[v] + cy[t + 1, v] for v in range(chunks)]
        west = [west_of_first(near[-1], levels)] + near[:-1]
        for v in range(chunks):
            ax[t, v] = jnp.abs(u[v]) - u[v] * u[v]
            bx[t, v] = 0.125 * u[v] * (near[v] + west[v])
        near = [u[v] + cx[t - 1, v] for v in range(chunks)]
        east = near[1:] + [east_of_last(near[0], levels)]
        for v in range(chunks):
            ay[t, v] = jnp.abs(w[v]) - w[v] * w[v]
            by[t, v] = 0.125 * w[v] * (near[v] + east[v])
        return carry

    lax.fori_loop(start, stop, factors, 0)


def own_courant_kernel(lon, lat, own, upper, lower, rows, turned, sem):
    levels, band, _ = lon.shape
    chunks = rows.shape[2]
    for start in range(0, band, SUB):

        def tiles_of(n, start=start):
            return [
                wind[level, start : start + SUB, lanes_of(part, n, turned.shape[0])]
                for wind in (lon, lat)
                for part in range(SUB // levels)
                for level in range(levels)
            ]

        turn(tiles_of, rows, start, turned)
    copy = pltpu.make_async_copy(rows, own, sem)
    copy.start()
    for out, start in ((upper, band - HALO + 1), (lower, 0)):
        for i in range(out.shape[0]):
            wind, t = halo_row(i)
            for v in range(0, chunks, 2):
                both = jnp.concatenate([rows[wind, start + t, v], rows[wind, start + t, v + 1]], 0)
                out[i, v * SUB : (v + 2) * SUB, :] = both.astype(BF16)
    copy.wait()


def halo_row(i):
    return divmod(i, HALO - 1) if i < 2 * HALO - 2 else (1, HALO - 1)


def own_courant(lon, lat):
    levels, band, nlon = lon.shape
    parts = SUB // levels
    chunks = nlon // (parts * LANES)
    shape = (2, band, chunks, SUB, LANES)
    far, vmem = pl.BlockSpec(memory_space=pltpu.HBM), pl.BlockSpec(memory_space=pltpu.VMEM)
    return pl.pallas_call(
        own_courant_kernel,
        out_shape=[
            pltpu.HBM(shape, F32),
            jax.ShapeDtypeStruct((2 * HALO - 2, chunks * SUB, LANES), BF16),
            jax.ShapeDtypeStruct((2 * HALO - 1, chunks * SUB, LANES), BF16),
        ],
        out_specs=[far, vmem, vmem],
        scratch_shapes=[
            pltpu.VMEM(shape, F32),
            pltpu.VMEM((chunks * LANES, LANES), F32),
            pltpu.SemaphoreType.DMA,
        ],
        compiler_params=params(16),
        name="own_courant",
    )(lon, lat)


def inner_kernel(levels, own, far_out, fields, sems):
    rows = fields.shape[1]
    copy = pltpu.make_async_copy(own, fields.at[pl.ds(0, 2)], sems.at[0])
    copy.start()
    copy.wait()
    add_factors(fields, levels, 1, rows - 1)
    copy = pltpu.make_async_copy(fields.at[:, pl.ds(1, rows - 2)], far_out, sems.at[1])
    copy.start()
    copy.wait()


def inner_fields(own, levels):
    _, band, chunks, _, _ = own.shape
    far = pl.BlockSpec(memory_space=pltpu.HBM)
    return pl.pallas_call(
        functools.partial(inner_kernel, levels),
        out_shape=pltpu.HBM((6, band - 2, chunks, SUB, LANES), F32),
        in_specs=[far],
        out_specs=far,
        scratch_shapes=[
            pltpu.VMEM((6, band, chunks, SUB, LANES), F32),
            pltpu.SemaphoreType.DMA((2,)),
        ],
        compiler_params=params(16),
        name="inner",
    )(pltpu.with_memory_space_constraint(own, pltpu.HBM))


def edge_kernel(levels, side, own, received, far_out, fields, sems):
    rows, chunks = fields.shape[1:3]
    band = own.shape[1]
    copy = pltpu.make_async_copy(
        own.at[:, pl.ds((band - 2) * side, 2)],
        fields.at[pl.ds(0, 2), pl.ds(0 if side else HALO, 2)],
        sems.at[0],
    )
    copy.start()
    for i in range(side, 6):
        fields[i, rows - 1 if side else 0] = jnp.zeros(fields.shape[2:], F32)
    if side:
        fields[0, rows - 1] = jnp.zeros(fields.shape[2:], F32)
    for i in range(received.shape[0]):
        wind, t = halo_row(i)
        for v in range(0, chunks, 2):
            both = received[i, v * SUB : (v + 2) * SUB, :].astype(F32)
            fields[wind, 1 + side + t, v] = both[:SUB]
            fields[wind, 1 + side + t, v + 1] = both[SUB:]
    copy.wait()
    middle = rows // 2
    spans = [
        (0, 2, side, HALO + 1),
        (2, 4, side, middle - side),
        (2, 4, middle, HALO + 1 + side - middle),
    ]
    copies = [
        pltpu.make_async_copy(
            fields.at[pl.ds(first, count), pl.ds(t, height)],
            far_out.at[pl.ds(first, count), pl.ds(t - side, height)],
            sems.at[1 + i],
        )
        for i, (first, count, t, height) in enumerate(spans)
    ]
    copies[0].start()
    add_factors(fields, levels, 1, middle)
    copies[1].start()
    add_factors(fields, levels, middle, rows - 1)
    copies[2].start()
    for copy in copies:
        copy.wait()


def edge_fields(own, received, side, levels):
    chunks = own.shape[2]
    vmem, far = pl.BlockSpec(memory_space=pltpu.VMEM), pl.BlockSpec(memory_space=pltpu.HBM)
    return pl.pallas_call(
        functools.partial(edge_kernel, levels, side),
        out_shape=pltpu.HBM((6, HALO + 1, chunks, SUB, LANES), F32),
        in_specs=[far, vmem],
        out_specs=far,
        scratch_shapes=[
            pltpu.VMEM((6, HALO + 2, chunks, SUB, LANES), F32),
            pltpu.SemaphoreType.DMA((4,)),
        ],
        compiler_params=params(16),
        cost_estimate=pl.CostEstimate(
            flops=6_000_000_000 if side else 1_000_000_000,
            bytes_accessed=8_000_000,
            transcendentals=0,
        ),
        name="edge",
    )(pltpu.with_memory_space_constraint(own, pltpu.HBM), received)


def spread(real, imag, count):
    def weighted(function, v, values, parity):
        total = None
        for m in range(parity, len(values), 2):
            factor = function(2.0 * math.pi * (m * v % count) / count)
            if abs(factor) > 1e-9:
                term = values[m] if abs(factor - 1.0) < 1e-9 else factor * values[m]
                total = term if total is None else total + term
        return total

    def add(x, y):
        return y if x is None else x if y is None else x + y

    def subtract(x, y):
        return x if y is None else -y if x is None else x - y

    half = count // 2
    out = [None] * count
    for v in range(half // 2 + 1):
        sums = [
            [weighted(function, v, values, parity) for parity in range(2)]
            for function, values in (
                (math.cos, real),
                (math.sin, imag),
                (math.cos, imag),
                (math.sin, real),
            )
        ]
        (p0, p1), (q0, q1), (r0, r1), (u0, u1) = sums
        found = [(v, add(p0, p1), add(q0, q1), add(r0, r1), add(u0, u1))]
        if v < half - v:
            found.append(
                (half - v, subtract(p0, p1), subtract(q1, q0), subtract(r0, r1), subtract(u1, u0))
            )
        for w, p, q, r, u in found:
            out[w] = (subtract(p, q), add(r, u))
            if 0 < w < half:
                out[count - w] = (add(p, q), subtract(r, u))
    return out


def transform(
    arrived, numbers, order, twist, table, lhs, mixed, terms, field, pad, levels
):
    sources = arrived.shape[0]
    rows, chunks = field.shape[:2]
    pieces = rows // SUB
    group = LANES // pad
    lane = lax.broadcasted_iota(jnp.int32, (SUB * SUB, LANES), 1)
    height = levels * SUB
    for g in range(-(-sources // group)):
        members = [arrived[q].astype(F32) for q in range(g * group, min(sources, (g + 1) * group))]
        for piece in range(pieces):
            value = None
            for i, member in enumerate(members):
                shift = pad * (i - piece) % LANES
                turned = pltpu.roll(member, shift, 1) if shift else member
                value = turned if value is None else jnp.where(lane >= i * pad, turned, value)
            value = value.astype(BF16)
            for c in range(2):
                first = (c * pieces + piece) * height
                lhs[first : first + height, g * LANES : (g + 1) * LANES] = value[
                    c * height : (c + 1) * height
                ]
    half = pieces * height
    near = table.shape[1]
    depth = mixed.shape[0]
    column = lax.broadcasted_iota(jnp.int32, (2 * SUB, LANES), 1)

    def one_hot(i, carry):
        span = pl.ds(pl.multiple_of(i * 2 * SUB, 2 * SUB), 2 * SUB)
        number = jnp.broadcast_to(numbers[span, :], (2 * SUB, LANES))
        weight = jnp.where(number == 0, 1.0, 2.0)
        for lo in range(0, order.shape[1], LANES):
            order[span, lo : lo + LANES] = jnp.where(column + lo == number, weight, 0.0).astype(BF16)
        return carry

    lax.fori_loop(0, order.shape[0] // (2 * SUB), one_hot, 0, unroll=4)
    for m in range(depth):
        mixed[m] = jnp.dot(
            lhs[...], order[:, m * near : (m + 1) * near], preferred_element_type=F32
        )

    def vary(i, carry):
        span = pl.ds(pl.multiple_of(i * 2 * SUB, 2 * SUB), 2 * SUB)
        other = pl.ds(pl.multiple_of(half + i * 2 * SUB, 2 * SUB), 2 * SUB)
        for lo in range(0, near, LANES):
            lanes = slice(lo, lo + LANES)
            real = [mixed[m, span, lanes] for m in range(depth)]
            imag = [mixed[m, other, lanes] for m in range(depth)]
            for v, (x, y) in enumerate(spread(real, imag, chunks)):
                if v:
                    cos, sin = twist[2 * v : 2 * v + 1, lanes], twist[2 * v + 1 : 2 * v + 2, lanes]
                    x, y = x * cos - y * sin, x * sin + y * cos
                for c, value in enumerate((x, y)):
                    high = value.astype(BF16)
                    low = (value - high.astype(F32)).astype(BF16)
                    terms[v, span, c * near + lo : c * near + lo + LANES] = high
                    terms[v, span, (2 + c) * near + lo : (2 + c) * near + lo + LANES] = low
        return carry

    lax.fori_loop(0, half // (2 * SUB), vary, 0)
    parts = SUB // levels

    group = chunks // 2

    def finish(i, carry):
        both = terms[pl.ds(i * group, group)].reshape(group * half, 4 * near)
        high, low = both[:, : 2 * near], both[:, 2 * near :]
        value = jnp.dot(high, table[: 2 * near], preferred_element_type=F32)
        value += jnp.dot(low, table[: 2 * near], preferred_element_type=F32)
        value += jnp.dot(high, table[2 * near :], preferred_element_type=F32)
        for v in range(group):
            for piece in range(pieces):
                tiles = []
                for part in range(parts):
                    for level in range(levels):
                        first = v * half + (piece * levels + level) * SUB
                        lanes = slice(part * LANES, (part + 1) * LANES)
                        tiles.append(value[first : first + SUB, lanes])
                turned = jnp.swapaxes(jnp.stack(tiles, 0), 0, 1)
                for t in range(SUB):
                    field[piece * SUB + t, i * group + v] = turned[t]
        return carry

    lax.fori_loop(0, chunks // group, finish, 0)


def donor(a, b, speed):
    return speed * jnp.where(speed > 0.0, a, b)


def upwind_rows(t, count, old, new, cx, cy, levels):
    chunks = old.shape[1]
    west = [west_of_first(old[t + r, chunks - 1], levels) for r in range(count)]
    first, base = None, None
    for v in range(chunks + 1):
        if v < chunks:
            q = [old[t - 1 + r, v] for r in range(count + 2)]
            flux_lat, flux_lon = [], []
            for r in range(count + 1):
                speed = cy[t + r, v]
                flux_lat.append(donor(q[r], q[r + 1], speed))
            for r in range(count):
                speed = cx[t + r, v]
                flux_lon.append(donor(west[r], q[r + 1], speed))
            west = q[1 : count + 1]
            first = flux_lon if v == 0 else first
        else:
            flux_lon = [east_of_last(x, levels) for x in first]
        for r in range(count):
            if v > 0:
                new[t + r, v - 1] = base[r] - flux_lon[r]
        if v < chunks:
            base = [q[r + 1] + flux_lon[r] - (flux_lat[r + 1] - flux_lat[r]) for r in range(count)]


def corrective_rows(t, count, old, new, ax, bx, ay, by, levels):
    chunks = old.shape[1]
    span = range(count + 2)

    def inverse(x):
        return pl.reciprocal(jnp.maximum(x, 1.0), approx=True)

    here = [old[t - 1 + r, 0] for r in span]
    start = here
    west = [west_of_first(old[t - 1 + r, chunks - 1], levels) for r in span]
    size, size_west = [jnp.abs(x) for x in here], [jnp.abs(x) for x in west]
    first, base = None, None
    for v in range(chunks + 1):
        if v < chunks:
            if v + 1 < chunks:
                east = [old[t - 1 + r, v + 1] for r in span]
            else:
                east = [east_of_last(x, levels) for x in start]
            size_east = [jnp.abs(x) for x in east]
            flux_lat, flux_lon = [], []
            apart = [east[r] - west[r] for r in span]
            sizes_apart = [size_east[r] + size_west[r] for r in span]
            for r in range(count + 1):
                step = here[r + 1] - here[r]
                gradient = step * inverse(size[r + 1] + size[r])
                cross = (apart[r + 1] + apart[r]) * inverse(sizes_apart[r + 1] + sizes_apart[r])
                speed = ay[t + r, v] * gradient - by[t + r, v] * cross
                flux_lat.append(donor(here[r], here[r + 1], speed))
            total = [here[r] + west[r] for r in span]
            sizes = [size[r] + size_west[r] for r in span]
            for r in range(1, count + 1):
                step = here[r] - west[r]
                gradient = step * inverse(sizes[r])
                cross = (total[r + 1] - total[r - 1]) * inverse(sizes[r + 1] + sizes[r - 1])
                speed = ax[t + r - 1, v] * gradient - bx[t + r - 1, v] * cross
                flux_lon.append(donor(west[r], here[r], speed))
            first = flux_lon if v == 0 else first
        else:
            flux_lon = [east_of_last(x, levels) for x in first]
        for r in range(count):
            if v > 0:
                new[t + r, v - 1] = base[r] - flux_lon[r]
        if v < chunks:
            base = [
                here[r + 1] + flux_lon[r] - (flux_lat[r + 1] - flux_lat[r]) for r in range(count)
            ]
            west, here, size_west, size = here, east, size, size_east


def advect_kernel(pad, arrived, numbers, twist, table, *refs):
    far_fields = refs[:3]
    out, fields, order, lhs, mixed, terms, field, upwind, turned, sems = refs[3:]
    cx, cy, ax, bx, ay, by = [fields.at[i] for i in range(6)]
    levels, band, nlon = out.shape
    rows, chunks = field.shape[:2]
    copies = []
    start = 0
    for i, far in enumerate(far_fields):
        place = fields.at[:, pl.ds(start, far.shape[1])]
        copies.append(pltpu.make_async_copy(far, place, sems.at[i]))
        start += far.shape[1]
    for copy in copies:
        copy.start()
    transform(arrived, numbers, order, twist, table, lhs, mixed, terms, field, pad, levels)
    for copy in copies:
        copy.wait()
    outermost = lax.axis_index("wave") == 0

    def clear(where):
        @pl.when(outermost)
        def _():
            where[HALO - 1] = jnp.zeros((chunks, SUB, LANES), F32)

    def one_pass(number):
        start, height = 2 * number + 1, rows // 2 - 1 - 2 * number

        def first(i, carry):
            upwind_rows(start + height * i, height, field, upwind, cx, cy, levels)
            return carry

        lax.fori_loop(0, 2, first, 0)
        clear(upwind)

        def second(i, carry):
            at = start + 1 + (height - 1) * i
            corrective_rows(at, height - 1, upwind, field, ax, bx, ay, by, levels)
            return carry

        lax.fori_loop(0, 2, second, 0)
        clear(field)

    for number in range(PASSES):
        one_pass(number)
    span = nlon * levels // SUB
    for block in range(band // SUB):
        first = HALO + block * SUB

        def stand(v, carry, first=first):
            value = jnp.swapaxes(field[pl.ds(first, SUB), v], 0, 1).reshape(SUB * SUB, LANES)
            value = jnp.transpose(jnp.concatenate([value, value], 0))
            turned[pl.ds(v, LANES, stride=chunks), :] = value
            return carry

        lax.fori_loop(0, chunks, stand, 0, unroll=2)
        for n in range(span // LANES):
            value = jnp.transpose(turned[n * LANES : (n + 1) * LANES, :])
            for i in range(SUB):
                lanes = i // levels * span + n * LANES
                out[i % levels, block * SUB : (block + 1) * SUB, lanes : lanes + LANES] = value[
                    i * SUB : (i + 1) * SUB
                ]


def advect(arrived, numbers, twist, table, fields, waves, shape, pad):
    levels, band, nlon = shape
    rows, chunks = sum(x.shape[1] for x in fields), fields[0].shape[2]
    half = rows * levels
    near = table.shape[1]
    fields = [pltpu.with_memory_space_constraint(x, pltpu.HBM) for x in fields]
    order = (numbers.shape[0], waves)
    vmem, far = pl.BlockSpec(memory_space=pltpu.VMEM), pl.BlockSpec(memory_space=pltpu.HBM)
    return pl.pallas_call(
        functools.partial(advect_kernel, pad),
        out_shape=jax.ShapeDtypeStruct(shape, F32),
        in_specs=[vmem] * 4 + [far] * 3,
        scratch_shapes=[
            pltpu.VMEM((6, rows, chunks, SUB, LANES), F32),
            pltpu.VMEM(order, BF16),
            pltpu.VMEM((2 * half, order[0]), BF16),
            pltpu.VMEM((waves // near, 2 * half, near), F32),
            pltpu.VMEM((chunks, half, 4 * near), BF16),
            pltpu.VMEM((rows, chunks, SUB, LANES), F32),
            pltpu.VMEM((rows, chunks, SUB, LANES), F32),
            pltpu.VMEM((nlon * levels // SUB, LANES), F32),
            pltpu.SemaphoreType.DMA((3,)),
        ],
        compiler_params=params(40),
        name="advect",
    )(arrived, numbers, twist, table, *fields)


def fourier_tables(nlon, near):
    chunks = nlon // near
    f = np.arange(near)
    angle = 2.0 * np.pi / nlon * (np.arange(chunks)[:, None] * f[None, :] % nlon)
    twist = np.stack([np.cos(angle), np.sin(angle)], 1).reshape(2 * chunks, near)
    angle = 2.0 * np.pi / near * (f[:, None] * f[None, :] % near)
    whole = np.concatenate([np.cos(angle), -np.sin(angle)], 0).astype(np.float32)
    high = whole.astype(ml_dtypes.bfloat16)
    low = (whole - high.astype(np.float32)).astype(ml_dtypes.bfloat16)
    return twist.astype(np.float32), np.concatenate([high, low], 0)


def arrival(wave_table, sources, pad):
    waves = 2 * wave_table.shape[0]
    group = LANES // pad
    numbers = jnp.stack([wave_table, waves - 1 - wave_table], 1).reshape(sources, -1)
    extra = -sources % group
    column = jnp.pad(numbers, ((0, extra), (0, pad - numbers.shape[1])), constant_values=-1)
    column = column.reshape(-1, group * pad)
    column = jnp.pad(column, ((0, 0), (0, LANES - group * pad)), constant_values=-1)
    column = column.reshape(-1, 1)
    return column


def body(spectral, legendre, wave_table, courant_lon, courant_lat):
    wave_count, level_count = lax.axis_size("wave"), lax.axis_size("lev")
    wave_rank, level_rank = lax.axis_index("wave"), lax.axis_index("lev")
    levels, band, nlon = courant_lon.shape
    own = legendre.shape[0]
    waves = 2 * wave_table.shape[0]
    pad = -(-2 * own // SUB) * SUB

    up = [(i, i + 1) for i in range(wave_count - 1)]
    down = [(i + 1, i) for i in range(wave_count - 1)]
    spectral = spectral.reshape((-1,) + spectral.shape[2:])
    half = level_count // 2
    far_blocks = pack(spectral, range(half, level_count), level_count)
    far_blocks, spectral = lax.optimization_barrier((far_blocks, spectral))
    blocks = list(pack(spectral, range(half), level_count)) + list(far_blocks)
    for step in range(1, level_count):
        pairs = [(i, i ^ step) for i in range(level_count)]
        blocks[step] = lax.ppermute(blocks[step], "lev", pairs)
    blocks[1], winds = lax.optimization_barrier((blocks[1], (courant_lon, courant_lat)))
    own_winds, upper, lower = own_courant(*winds)
    below = lax.ppermute(upper, "wave", up)
    above = lax.ppermute(lower, "wave", down)

    own_pairs = lax.dynamic_slice_in_dim(
        wave_table, (wave_rank * level_count + level_rank) * own, own
    )
    turned = jnp.swapaxes(legendre, 1, 2)
    given = (turned, own_pairs, wave_count, waves, pad)
    sums = list(legendre_sums(range(level_count - 1), blocks[:-1], *given))
    numbers = arrival(wave_table, wave_count * level_count, pad)
    stacked = legendre_sums([level_count - 1], blocks[-1:], *given, done=tuple(sums))
    arrived = lax.all_to_all(
        stacked.reshape(-1, SUB * SUB, LANES), ("wave", "lev"), 0, 0, tiled=True
    )

    fields = [
        edge_fields(own_winds, below, 0, levels),
        inner_fields(own_winds, levels),
        edge_fields(own_winds, above, 1, levels),
    ]
    twist, table = fourier_tables(nlon, SUB // levels * LANES)
    return advect(
        arrived, numbers, jnp.asarray(twist), jnp.asarray(table), fields, waves, courant_lon.shape, pad
    )


def solution(mesh):
    placed = (
        P(None, "lev", "wave", None),
        P(("wave", "lev"), None, None),
        P(),
        P("lev", "wave", None),
        P("lev", "wave", None),
    )
    return jax.shard_map(
        body, mesh=mesh, in_specs=placed, out_specs=P("lev", "wave", None), check_vma=False
    )
```

```python
import functools
import math

import jax
import jax.numpy as jnp
import ml_dtypes
import numpy as np
from jax import lax
from jax.experimental import pallas as pl
from jax.experimental.pallas import tpu as pltpu
from jax.sharding import PartitionSpec as P

PASSES = 4
HALO = 2 * PASSES
SUB = 8
LANES = 128
F32 = jnp.float32
BF16 = jnp.bfloat16


def params(mib):
    return pltpu.CompilerParams(vmem_limit_bytes=mib << 20)


def lane_index():
    return lax.broadcasted_iota(jnp.int32, (SUB, LANES), 1)


def pack_kernel(count, steps, x_ref, *refs):
    turned = refs[-1]
    degrees = x_ref.shape[2]
    own = turned.shape[0] // (count // 2)
    pairs = -(-own // 2)
    whole = degrees // LANES
    me = lax.axis_index("lev")
    there = (me ^ steps[0]) // (count // 2)
    for part in range(2):
        start = part * turned.shape[0]
        first = start // SUB * SUB

        @pl.when(there == part)
        def _(start=start, first=first):
            for group in range(first, start + turned.shape[0], SUB):
                for lo in range(0, degrees, LANES):
                    hi = min(lo + LANES, degrees)
                    tile = [x_ref[i, group : group + SUB, lo:hi].astype(F32) for i in range(SUB)]
                    tile = jnp.swapaxes(jnp.stack(tile, 0), 0, 1)
                    skip = max(start - group, 0)
                    keep = min(start + turned.shape[0] - group, SUB)
                    at = group + skip - start
                    turned[at : at + keep - skip, :, lo:hi] = tile[skip:keep]

    lane = lax.broadcasted_iota(jnp.int32, (2 * SUB, LANES), 1)
    for step, out in zip(steps, refs):
        start = (me ^ step) % (count // 2) * own

        def two(i, start=start):
            return start + 2 * i, start + jnp.minimum(2 * i + 1, own - 1)

        def pair(i, carry, out=out, two=two):
            for n in range(whole):
                both = [turned[slot, :, n * LANES : (n + 1) * LANES] for slot in two(i)]
                row = pl.multiple_of((i * whole + n) * 2 * SUB, 2 * SUB)
                out[pl.ds(row, 2 * SUB), :] = jnp.concatenate(both, 0).astype(BF16)
            return carry

        lax.fori_loop(0, pairs, pair, 0)
        rest = jnp.zeros((2 * SUB, LANES), F32)
        for i in range(pairs):
            last = [turned[slot, :, whole * LANES :] for slot in two(i)]
            rest = jnp.where(lane == i, jnp.concatenate(last, 0), rest)
        out[pairs * whole * 2 * SUB :, :] = rest.astype(BF16)


def pack(spectral, steps, count):
    levels, slots, degrees = spectral.shape
    pairs = -(-slots // count // 2)
    out = jax.ShapeDtypeStruct(((pairs * (degrees // LANES) + 1) * 2 * SUB, LANES), BF16)
    spectral = jnp.pad(spectral, ((0, 0), (0, -slots % (2 * SUB)), (0, 0)))
    return pl.pallas_call(
        functools.partial(pack_kernel, count, steps),
        out_shape=[out] * len(steps),
        scratch_shapes=[pltpu.VMEM((slots // 2, SUB, degrees), F32)],
        compiler_params=params(40),
        name="pack",
    )(spectral)


def legendre_kernel(steps, bands, waves, pad, early, pairs_ref, *refs):
    count = len(steps)
    blocks, table, done = refs[:count], refs[count], refs[count + 1 : count + 1 + early]
    outs, sums = refs[count + 1 + early : -1], refs[-1]
    if early:
        me = lax.axis_index("lev")
        outs = [outs[0].at[:, me ^ step] for step in range(early + count)]
        for value, out in zip(done, outs):
            out[...] = value[...]
        outs = outs[early:]
    own, lats, degrees = table.shape
    whole = degrees // LANES
    wide = sums.shape[-1]
    band = lats // bands
    pieces = band // SUB + 2
    if wide > lats:
        sums[...] = jnp.zeros_like(sums)
    elif 2 * own < pad:
        sums[:, 2 * own :] = jnp.zeros((count, pad - 2 * own, SUB, wide), F32)

    def pair(i, carry):
        rows = []
        for block in blocks:
            parts = []
            for n in range(whole):
                first = pl.multiple_of((i * whole + n) * 2 * SUB, 2 * SUB)
                parts.append(block[pl.ds(first, 2 * SUB), :].astype(F32))
            rest = block[block.shape[0] - 2 * SUB :, :].astype(F32)
            parts.append(pltpu.roll(rest, (LANES - i) % LANES, 1)[:, : degrees - whole * LANES])
            rows.append(jnp.concatenate(parts, 1))
        rows = jnp.concatenate(rows, 0)
        row = lax.broadcasted_iota(jnp.int32, rows.shape, 0) % (2 * SUB)
        degree = lax.broadcasted_iota(jnp.int32, rows.shape, 1)
        second = jnp.minimum(2 * i + 1, own - 1)
        bound = waves - jnp.where(row < SUB, pairs_ref[2 * i], pairs_ref[second])
        low = jnp.where(degree < bound, rows, 0.0)
        both = jnp.concatenate([low, rows - low], 0).astype(BF16)
        for j in range(2):
            got = lax.dot_general(
                both,
                table[second if j else 2 * i],
                (((1,), (1,)), ((), ())),
                preferred_element_type=F32,
            )
            for half in range(2):
                for d in range(count):
                    first = (half * count + d) * 2 * SUB + j * SUB
                    sums[d, 4 * i + 2 * j + half, :, :lats] = got[first : first + SUB]
        return carry

    lax.fori_loop(0, -(-own // 2), pair, 0, unroll=10)
    lane = lane_index()
    nothing = jnp.zeros((SUB, LANES), F32)
    for d in range(count):
        tiles = [
            [jnp.swapaxes(sums[d, 8 * g : 8 * g + 8, :, k : k + LANES], 0, 1) for k in range(0, wide, LANES)]
            for g in range(pad // SUB)
        ]
        stood = []
        for i in range(SUB):
            once = [jnp.concatenate([tile[i] for tile in row], 1) for row in tiles]
            spare = (LANES - pieces * pad) // SUB
            tall = once * pieces + [jnp.zeros((SUB, wide), F32)] * spare
            stood.append(jnp.transpose(jnp.concatenate(tall, 0)))
        for w in range(bands):
            for i in range(0, SUB, 2):
                two = []
                for value in stood[i : i + 2]:
                    tile = nothing
                    for piece in reversed(range(pieces)):
                        first = w * band + (piece - 1) * SUB
                        there = value[first : first + SUB] if 0 <= first < lats else nothing
                        tile = there if piece == pieces - 1 else jnp.where(
                            lane < (piece + 1) * pad, there, tile
                        )
                    two.append(tile)
                outs[d][w, i * SUB : (i + 2) * SUB, :] = jnp.concatenate(two, 0).astype(BF16)


def legendre_sums(steps, blocks, table, own_pairs, bands, waves, pad, done=()):
    own, lats, degrees = table.shape
    wide = -(-lats // LANES) * LANES
    outs = [jax.ShapeDtypeStruct((bands, SUB * SUB, LANES), BF16)] * len(steps)
    if done:
        outs = jax.ShapeDtypeStruct((bands, len(done) + len(steps), SUB * SUB, LANES), BF16)
    vmem = pl.BlockSpec(memory_space=pltpu.VMEM)
    return pl.pallas_call(
        functools.partial(legendre_kernel, steps, bands, waves, pad, len(done)),
        out_shape=outs,
        in_specs=[pl.BlockSpec(memory_space=pltpu.SMEM)] + [vmem] * (len(steps) + 1 + len(done)),
        scratch_shapes=[pltpu.VMEM((len(steps), pad, SUB, wide), F32)],
        compiler_params=params(40),
        name="legendre",
    )(own_pairs, *blocks, table, *done)


def west_of_first(last_chunk, levels):
    turned = pltpu.roll(last_chunk, 1, 1)
    return jnp.where(lane_index() == 0, pltpu.roll(turned, levels, 0), turned)


def east_of_last(first_chunk, levels):
    turned = pltpu.roll(first_chunk, LANES - 1, 1)
    return jnp.where(lane_index() == LANES - 1, pltpu.roll(turned, SUB - levels, 0), turned)


def turn(tiles_of, rows, start, turned):
    chunks = rows.shape[2]

    def stand(n, carry):
        first = pl.multiple_of(n * LANES, LANES)
        turned[pl.ds(first, LANES), :] = jnp.transpose(jnp.concatenate(tiles_of(n), 0))
        return carry

    def lie(v, carry):
        value = jnp.transpose(turned[pl.ds(v, LANES, stride=chunks), :])
        for field in range(2):
            both = value[field * SUB * SUB : (field + 1) * SUB * SUB]
            both = jnp.swapaxes(both.reshape(SUB, SUB, LANES), 0, 1)
            for t in range(SUB):
                rows[field, start + t, v] = both[t]
        return carry

    lax.fori_loop(0, turned.shape[0] // LANES, stand, 0, unroll=4)
    lax.fori_loop(0, chunks, lie, 0, unroll=4)


def lanes_of(part, n, span):
    return pl.ds(pl.multiple_of(part * span + n * LANES, LANES), LANES)


def add_factors(fields, levels, start, stop):
    cx, cy, ax, bx, ay, by = [fields.at[i] for i in range(6)]
    chunks = fields.shape[2]

    def factors(t, carry):
        u = [cx[t, v] for v in range(chunks)]
        w = [cy[t, v] for v in range(chunks)]
        near = [w[v] + cy[t + 1, v] for v in range(chunks)]
        west = [west_of_first(near[-1], levels)] + near[:-1]
        for v in range(chunks):
            ax[t, v] = jnp.abs(u[v]) - u[v] * u[v]
            bx[t, v] = 0.125 * u[v] * (near[v] + west[v])
        near = [u[v] + cx[t - 1, v] for v in range(chunks)]
        east = near[1:] + [east_of_last(near[0], levels)]
        for v in range(chunks):
            ay[t, v] = jnp.abs(w[v]) - w[v] * w[v]
            by[t, v] = 0.125 * w[v] * (near[v] + east[v])
        return carry

    lax.fori_loop(start, stop, factors, 0, unroll=4)


def own_courant_kernel(lon, lat, own, upper, lower, rows, turned, sem):
    levels, band, _ = lon.shape
    chunks = rows.shape[2]
    for start in range(0, band, SUB):

        def tiles_of(n, start=start):
            return [
                wind[level, start : start + SUB, lanes_of(part, n, turned.shape[0])]
                for wind in (lon, lat)
                for part in range(SUB // levels)
                for level in range(levels)
            ]

        turn(tiles_of, rows, start, turned)
    copy = pltpu.make_async_copy(rows, own, sem)
    copy.start()
    for out, start in ((upper, band - HALO + 1), (lower, 0)):
        for i in range(out.shape[0]):
            wind, t = halo_row(i)
            for v in range(0, chunks, 2):
                both = jnp.concatenate([rows[wind, start + t, v], rows[wind, start + t, v + 1]], 0)
                out[i, v * SUB : (v + 2) * SUB, :] = both.astype(BF16)
    copy.wait()


def halo_row(i):
    return divmod(i, HALO - 1) if i < 2 * HALO - 2 else (1, HALO - 1)


def own_courant(lon, lat):
    levels, band, nlon = lon.shape
    parts = SUB // levels
    chunks = nlon // (parts * LANES)
    shape = (2, band, chunks, SUB, LANES)
    far, vmem = pl.BlockSpec(memory_space=pltpu.HBM), pl.BlockSpec(memory_space=pltpu.VMEM)
    return pl.pallas_call(
        own_courant_kernel,
        out_shape=[
            pltpu.HBM(shape, F32),
            jax.ShapeDtypeStruct((2 * HALO - 2, chunks * SUB, LANES), BF16),
            jax.ShapeDtypeStruct((2 * HALO - 1, chunks * SUB, LANES), BF16),
        ],
        out_specs=[far, vmem, vmem],
        scratch_shapes=[
            pltpu.VMEM(shape, F32),
            pltpu.VMEM((chunks * LANES, LANES), F32),
            pltpu.SemaphoreType.DMA,
        ],
        compiler_params=params(16),
        name="own_courant",
    )(lon, lat)


def inner_kernel(levels, own, far_out, fields, sems):
    rows = fields.shape[1]
    copy = pltpu.make_async_copy(own, fields.at[pl.ds(0, 2)], sems.at[0])
    copy.start()
    copy.wait()
    add_factors(fields, levels, 1, rows - 1)
    copy = pltpu.make_async_copy(fields.at[:, pl.ds(1, rows - 2)], far_out, sems.at[1])
    copy.start()
    copy.wait()


def inner_fields(own, levels):
    _, band, chunks, _, _ = own.shape
    far = pl.BlockSpec(memory_space=pltpu.HBM)
    return pl.pallas_call(
        functools.partial(inner_kernel, levels),
        out_shape=pltpu.HBM((6, band - 2, chunks, SUB, LANES), F32),
        in_specs=[far],
        out_specs=far,
        scratch_shapes=[
            pltpu.VMEM((6, band, chunks, SUB, LANES), F32),
            pltpu.SemaphoreType.DMA((2,)),
        ],
        compiler_params=params(16),
        name="inner",
    )(pltpu.with_memory_space_constraint(own, pltpu.HBM))


def edge_kernel(levels, side, own, received, far_out, fields, sems):
    rows, chunks = fields.shape[1:3]
    band = own.shape[1]
    copy = pltpu.make_async_copy(
        own.at[:, pl.ds((band - 2) * side, 2)],
        fields.at[pl.ds(0, 2), pl.ds(0 if side else HALO, 2)],
        sems.at[0],
    )
    copy.start()
    for i in range(side, 6):
        fields[i, rows - 1 if side else 0] = jnp.zeros(fields.shape[2:], F32)
    if side:
        fields[0, rows - 1] = jnp.zeros(fields.shape[2:], F32)
    for i in range(received.shape[0]):
        wind, t = halo_row(i)
        for v in range(0, chunks, 2):
            both = received[i, v * SUB : (v + 2) * SUB, :].astype(F32)
            fields[wind, 1 + side + t, v] = both[:SUB]
            fields[wind, 1 + side + t, v + 1] = both[SUB:]
    copy.wait()
    middle = rows // 2
    spans = [
        (0, 2, side, HALO + 1),
        (2, 4, side, middle - side),
        (2, 4, middle, HALO + 1 + side - middle),
    ]
    copies = [
        pltpu.make_async_copy(
            fields.at[pl.ds(first, count), pl.ds(t, height)],
            far_out.at[pl.ds(first, count), pl.ds(t - side, height)],
            sems.at[1 + i],
        )
        for i, (first, count, t, height) in enumerate(spans)
    ]
    copies[0].start()
    add_factors(fields, levels, 1, middle)
    copies[1].start()
    add_factors(fields, levels, middle, rows - 1)
    copies[2].start()
    for copy in copies:
        copy.wait()


def edge_fields(own, received, side, levels):
    chunks = own.shape[2]
    vmem, far = pl.BlockSpec(memory_space=pltpu.VMEM), pl.BlockSpec(memory_space=pltpu.HBM)
    return pl.pallas_call(
        functools.partial(edge_kernel, levels, side),
        out_shape=pltpu.HBM((6, HALO + 1, chunks, SUB, LANES), F32),
        in_specs=[far, vmem],
        out_specs=far,
        scratch_shapes=[
            pltpu.VMEM((6, HALO + 2, chunks, SUB, LANES), F32),
            pltpu.SemaphoreType.DMA((4,)),
        ],
        compiler_params=params(16),
        cost_estimate=pl.CostEstimate(
            flops=6_000_000_000 if side else 1_000_000_000,
            bytes_accessed=8_000_000,
            transcendentals=0,
        ),
        name="edge",
    )(pltpu.with_memory_space_constraint(own, pltpu.HBM), received)


def spread(real, imag, count):
    def weighted(function, v, values, parity):
        total = None
        for m in range(parity, len(values), 2):
            factor = function(2.0 * math.pi * (m * v % count) / count)
            if abs(factor) > 1e-9:
                term = values[m] if abs(factor - 1.0) < 1e-9 else factor * values[m]
                total = term if total is None else total + term
        return total

    def add(x, y):
        return y if x is None else x if y is None else x + y

    def subtract(x, y):
        return x if y is None else -y if x is None else x - y

    half = count // 2
    out = [None] * count
    for v in range(half // 2 + 1):
        sums = [
            [weighted(function, v, values, parity) for parity in range(2)]
            for function, values in (
                (math.cos, real),
                (math.sin, imag),
                (math.cos, imag),
                (math.sin, real),
            )
        ]
        (p0, p1), (q0, q1), (r0, r1), (u0, u1) = sums
        found = [(v, add(p0, p1), add(q0, q1), add(r0, r1), add(u0, u1))]
        if v < half - v:
            found.append(
                (half - v, subtract(p0, p1), subtract(q1, q0), subtract(r0, r1), subtract(u1, u0))
            )
        for w, p, q, r, u in found:
            out[w] = (subtract(p, q), add(r, u))
            if 0 < w < half:
                out[count - w] = (add(p, q), subtract(r, u))
    return out


def transform(
    arrived, numbers, order, twist, table, lhs, mixed, terms, field, pad, levels
):
    sources = arrived.shape[0]
    rows, chunks = field.shape[:2]
    pieces = rows // SUB
    group = LANES // pad
    lane = lax.broadcasted_iota(jnp.int32, (SUB * SUB, LANES), 1)
    height = levels * SUB
    for g in range(-(-sources // group)):
        members = [arrived[q].astype(F32) for q in range(g * group, min(sources, (g + 1) * group))]
        for piece in range(pieces):
            value = None
            for i, member in enumerate(members):
                shift = pad * (i - piece) % LANES
                turned = pltpu.roll(member, shift, 1) if shift else member
                value = turned if value is None else jnp.where(lane >= i * pad, turned, value)
            value = value.astype(BF16)
            for c in range(2):
                first = (c * pieces + piece) * height
                lhs[first : first + height, g * LANES : (g + 1) * LANES] = value[
                    c * height : (c + 1) * height
                ]
    half = pieces * height
    near = table.shape[1]
    depth = mixed.shape[0]
    column = lax.broadcasted_iota(jnp.int32, (2 * SUB, LANES), 1)

    def one_hot(i, carry):
        span = pl.ds(pl.multiple_of(i * 2 * SUB, 2 * SUB), 2 * SUB)
        number = jnp.broadcast_to(numbers[span, :], (2 * SUB, LANES))
        weight = jnp.where(number == 0, 1.0, 2.0)
        for lo in range(0, order.shape[1], LANES):
            order[span, lo : lo + LANES] = jnp.where(column + lo == number, weight, 0.0).astype(BF16)
        return carry

    lax.fori_loop(0, order.shape[0] // (2 * SUB), one_hot, 0, unroll=44)
    for m in range(depth):
        mixed[m] = jnp.dot(
            lhs[...], order[:, m * near : (m + 1) * near], preferred_element_type=F32
        )

    def vary(i, carry):
        span = pl.ds(pl.multiple_of(i * 2 * SUB, 2 * SUB), 2 * SUB)
        other = pl.ds(pl.multiple_of(half + i * 2 * SUB, 2 * SUB), 2 * SUB)
        for lo in range(0, near, LANES):
            lanes = slice(lo, lo + LANES)
            real = [mixed[m, span, lanes] for m in range(depth)]
            imag = [mixed[m, other, lanes] for m in range(depth)]
            for v, (x, y) in enumerate(spread(real, imag, chunks)):
                if v:
                    cos, sin = twist[2 * v : 2 * v + 1, lanes], twist[2 * v + 1 : 2 * v + 2, lanes]
                    x, y = x * cos - y * sin, x * sin + y * cos
                for c, value in enumerate((x, y)):
                    terms[v, span, c * near + lo : c * near + lo + LANES] = value.astype(BF16)
        return carry

    lax.fori_loop(0, half // (2 * SUB), vary, 0)
    parts = SUB // levels

    group = chunks // 2

    def finish(i, carry):
        both = terms[pl.ds(i * group, group)].reshape(group * half, 2 * near)
        value = jnp.dot(both, table[: 2 * near], preferred_element_type=F32)
        value += jnp.dot(both, table[2 * near :], preferred_element_type=F32)
        for v in range(group):
            for piece in range(pieces):
                tiles = []
                for part in range(parts):
                    for level in range(levels):
                        first = v * half + (piece * levels + level) * SUB
                        lanes = slice(part * LANES, (part + 1) * LANES)
                        tiles.append(value[first : first + SUB, lanes])
                turned = jnp.swapaxes(jnp.stack(tiles, 0), 0, 1)
                for t in range(SUB):
                    field[piece * SUB + t, i * group + v] = turned[t]
        return carry

    lax.fori_loop(0, chunks // group, finish, 0)


def donor(a, b, speed):
    return speed * jnp.where(speed > 0.0, a, b)


def upwind_rows(t, count, old, new, cx, cy, levels):
    chunks = old.shape[1]
    west = [west_of_first(old[t + r, chunks - 1], levels) for r in range(count)]
    first, base = None, None
    for v in range(chunks + 1):
        if v < chunks:
            q = [old[t - 1 + r, v] for r in range(count + 2)]
            flux_lat, flux_lon = [], []
            for r in range(count + 1):
                speed = cy[t + r, v]
                flux_lat.append(donor(q[r], q[r + 1], speed))
            for r in range(count):
                speed = cx[t + r, v]
                flux_lon.append(donor(west[r], q[r + 1], speed))
            west = q[1 : count + 1]
            first = flux_lon if v == 0 else first
        else:
            flux_lon = [east_of_last(x, levels) for x in first]
        for r in range(count):
            if v > 0:
                new[t + r, v - 1] = base[r] - flux_lon[r]
        if v < chunks:
            base = [q[r + 1] + flux_lon[r] - (flux_lat[r + 1] - flux_lat[r]) for r in range(count)]


def corrective_rows(t, count, old, new, ax, bx, ay, by, levels):
    chunks = old.shape[1]
    span = range(count + 2)

    def inverse(x):
        return pl.reciprocal(jnp.maximum(x, 1.0), approx=True)

    here = [old[t - 1 + r, 0] for r in span]
    start = here
    west = [west_of_first(old[t - 1 + r, chunks - 1], levels) for r in span]
    size, size_west = [jnp.abs(x) for x in here], [jnp.abs(x) for x in west]
    first, base = None, None
    for v in range(chunks + 1):
        if v < chunks:
            if v + 1 < chunks:
                east = [old[t - 1 + r, v + 1] for r in span]
            else:
                east = [east_of_last(x, levels) for x in start]
            size_east = [jnp.abs(x) for x in east]
            flux_lat, flux_lon = [], []
            apart = [east[r] - west[r] for r in span]
            sizes_apart = [size_east[r] + size_west[r] for r in span]
            for r in range(count + 1):
                step = here[r + 1] - here[r]
                gradient = step * inverse(size[r + 1] + size[r])
                cross = (apart[r + 1] + apart[r]) * inverse(sizes_apart[r + 1] + sizes_apart[r])
                speed = ay[t + r, v] * gradient - by[t + r, v] * cross
                flux_lat.append(donor(here[r], here[r + 1], speed))
            total = [here[r] + west[r] for r in span]
            sizes = [size[r] + size_west[r] for r in span]
            for r in range(1, count + 1):
                step = here[r] - west[r]
                gradient = step * inverse(sizes[r])
                cross = (total[r + 1] - total[r - 1]) * inverse(sizes[r + 1] + sizes[r - 1])
                speed = ax[t + r - 1, v] * gradient - bx[t + r - 1, v] * cross
                flux_lon.append(donor(west[r], here[r], speed))
            first = flux_lon if v == 0 else first
        else:
            flux_lon = [east_of_last(x, levels) for x in first]
        for r in range(count):
            if v > 0:
                new[t + r, v - 1] = base[r] - flux_lon[r]
        if v < chunks:
            base = [
                here[r + 1] + flux_lon[r] - (flux_lat[r + 1] - flux_lat[r]) for r in range(count)
            ]
            west, here, size_west, size = here, east, size, size_east


def advect_kernel(pad, arrived, numbers, twist, table, *refs):
    far_fields = refs[:3]
    out, fields, order, lhs, mixed, terms, field, upwind, turned, sems = refs[3:]
    cx, cy, ax, bx, ay, by = [fields.at[i] for i in range(6)]
    levels, band, nlon = out.shape
    rows, chunks = field.shape[:2]
    copies = []
    start = 0
    for i, far in enumerate(far_fields):
        place = fields.at[:, pl.ds(start, far.shape[1])]
        copies.append(pltpu.make_async_copy(far, place, sems.at[i]))
        start += far.shape[1]
    for copy in copies:
        copy.start()
    transform(arrived, numbers, order, twist, table, lhs, mixed, terms, field, pad, levels)
    for copy in copies:
        copy.wait()
    outermost = lax.axis_index("wave") == 0

    def clear(where):
        @pl.when(outermost)
        def _():
            where[HALO - 1] = jnp.zeros((chunks, SUB, LANES), F32)

    def one_pass(number):
        start, height = 2 * number + 1, rows // 2 - 1 - 2 * number

        def first(i, carry):
            upwind_rows(start + height * i, height, field, upwind, cx, cy, levels)
            return carry

        lax.fori_loop(0, 2, first, 0)
        clear(upwind)

        def second(i, carry):
            at = start + 1 + (height - 1) * i
            corrective_rows(at, height - 1, upwind, field, ax, bx, ay, by, levels)
            return carry

        lax.fori_loop(0, 2, second, 0)
        clear(field)

    for number in range(PASSES):
        one_pass(number)
    span = nlon * levels // SUB
    for block in range(band // SUB):
        first = HALO + block * SUB

        def stand(v, carry, first=first):
            value = jnp.swapaxes(field[pl.ds(first, SUB), v], 0, 1).reshape(SUB * SUB, LANES)
            value = jnp.transpose(jnp.concatenate([value, value], 0))
            turned[pl.ds(v, LANES, stride=chunks), :] = value
            return carry

        lax.fori_loop(0, chunks, stand, 0, unroll=20)
        for n in range(span // LANES):
            value = jnp.transpose(turned[n * LANES : (n + 1) * LANES, :])
            for i in range(SUB):
                lanes = i // levels * span + n * LANES
                out[i % levels, block * SUB : (block + 1) * SUB, lanes : lanes + LANES] = value[
                    i * SUB : (i + 1) * SUB
                ]


def advect(arrived, numbers, twist, table, fields, waves, shape, pad):
    levels, band, nlon = shape
    rows, chunks = sum(x.shape[1] for x in fields), fields[0].shape[2]
    half = rows * levels
    near = table.shape[1]
    fields = [pltpu.with_memory_space_constraint(x, pltpu.HBM) for x in fields]
    order = (numbers.shape[0], waves)
    vmem, far = pl.BlockSpec(memory_space=pltpu.VMEM), pl.BlockSpec(memory_space=pltpu.HBM)
    return pl.pallas_call(
        functools.partial(advect_kernel, pad),
        out_shape=jax.ShapeDtypeStruct(shape, F32),
        in_specs=[vmem] * 4 + [far] * 3,
        scratch_shapes=[
            pltpu.VMEM((6, rows, chunks, SUB, LANES), F32),
            pltpu.VMEM(order, BF16),
            pltpu.VMEM((2 * half, order[0]), BF16),
            pltpu.VMEM((waves // near, 2 * half, near), F32),
            pltpu.VMEM((chunks, half, 2 * near), BF16),
            pltpu.VMEM((rows, chunks, SUB, LANES), F32),
            pltpu.VMEM((rows, chunks, SUB, LANES), F32),
            pltpu.VMEM((nlon * levels // SUB, LANES), F32),
            pltpu.SemaphoreType.DMA((3,)),
        ],
        compiler_params=params(40),
        name="advect",
    )(arrived, numbers, twist, table, *fields)


def fourier_tables(nlon, near):
    chunks = nlon // near
    f = np.arange(near)
    angle = 2.0 * np.pi / nlon * (np.arange(chunks)[:, None] * f[None, :] % nlon)
    twist = np.stack([np.cos(angle), np.sin(angle)], 1).reshape(2 * chunks, near)
    angle = 2.0 * np.pi / near * (f[:, None] * f[None, :] % near)
    whole = np.concatenate([np.cos(angle), -np.sin(angle)], 0).astype(np.float32)
    high = whole.astype(ml_dtypes.bfloat16)
    low = (whole - high.astype(np.float32)).astype(ml_dtypes.bfloat16)
    return twist.astype(np.float32), np.concatenate([high, low], 0)


def arrival(wave_table, sources, pad):
    waves = 2 * wave_table.shape[0]
    group = LANES // pad
    numbers = jnp.stack([wave_table, waves - 1 - wave_table], 1).reshape(sources, -1)
    extra = -sources % group
    column = jnp.pad(numbers, ((0, extra), (0, pad - numbers.shape[1])), constant_values=-1)
    column = column.reshape(-1, group * pad)
    column = jnp.pad(column, ((0, 0), (0, LANES - group * pad)), constant_values=-1)
    column = column.reshape(-1, 1)
    return column


def body(spectral, legendre, wave_table, courant_lon, courant_lat):
    wave_count, level_count = lax.axis_size("wave"), lax.axis_size("lev")
    wave_rank, level_rank = lax.axis_index("wave"), lax.axis_index("lev")
    levels, band, nlon = courant_lon.shape
    own = legendre.shape[0]
    waves = 2 * wave_table.shape[0]
    pad = -(-2 * own // SUB) * SUB

    up = [(i, i + 1) for i in range(wave_count - 1)]
    down = [(i + 1, i) for i in range(wave_count - 1)]
    spectral = spectral.reshape((-1,) + spectral.shape[2:])
    half = level_count // 2
    far_blocks = pack(spectral, range(half, level_count), level_count)
    far_blocks, spectral = lax.optimization_barrier((far_blocks, spectral))
    blocks = list(pack(spectral, range(half), level_count)) + list(far_blocks)
    for step in range(1, level_count):
        pairs = [(i, i ^ step) for i in range(level_count)]
        blocks[step] = lax.ppermute(blocks[step], "lev", pairs)
    blocks[1], winds = lax.optimization_barrier((blocks[1], (courant_lon, courant_lat)))
    own_winds, upper, lower = own_courant(*winds)
    below = lax.ppermute(upper, "wave", up)
    above = lax.ppermute(lower, "wave", down)

    own_pairs = lax.dynamic_slice_in_dim(
        wave_table, (wave_rank * level_count + level_rank) * own, own
    )
    turned = jnp.swapaxes(legendre, 1, 2)
    given = (turned, own_pairs, wave_count, waves, pad)
    sums = list(legendre_sums(range(level_count - 1), blocks[:-1], *given))
    numbers = arrival(wave_table, wave_count * level_count, pad)
    stacked = legendre_sums([level_count - 1], blocks[-1:], *given, done=tuple(sums))
    arrived = lax.all_to_all(
        stacked.reshape(-1, SUB * SUB, LANES), ("wave", "lev"), 0, 0, tiled=True
    )

    fields = [
        edge_fields(own_winds, below, 0, levels),
        inner_fields(own_winds, levels),
        edge_fields(own_winds, above, 1, levels),
    ]
    twist, table = fourier_tables(nlon, SUB // levels * LANES)
    return advect(
        arrived, numbers, jnp.asarray(twist), jnp.asarray(table), fields, waves, courant_lon.shape, pad
    )


def solution(mesh):
    placed = (
        P(None, "lev", "wave", None),
        P(("wave", "lev"), None, None),
        P(),
        P("lev", "wave", None),
        P("lev", "wave", None),
    )
    return jax.shard_map(
        body, mesh=mesh, in_specs=placed, out_specs=P("lev", "wave", None), check_vma=False
    )
```
